32 devices in a mesh: lat: 8 (over z, x), depth: 4 (over y, core).
Axes of the slice: x: 2, y: 2, z: 4, core: 2. Of those that a mesh axis runs over, the one named last changes fastest.
Arguments:
- head: float32 [64, 64, 4096], P('depth', 'lat'), may hold values from -1 to 0.5
- head_old: float32 [64, 64, 4096], P('depth', 'lat'), may hold values from -1 to 0.5
- soil: int32 [64, 64, 4096], P('depth', 'lat'), may hold values from 0 to 11
- cond_table: float32 [12], replicated, may hold values from 0.3 to 2
- shape_table: float32 [12], replicated, may hold values from 0.3 to 1.5
- pore_table: float32 [12], replicated, may hold values from 0.2 to 0.5
- pond: float32 [64, 4096], P('lat'), may hold values from 0.02 to 0.6
- ground: float32 [64, 4096], P('lat'), may hold values from -1.5 to 1.5
- ponded: int32 [64, 4096], P('lat'), may hold values 0 or 1
- river: int32 [64, 4096], P('lat'), may hold values 0 or 1
Outputs:
- head_new: float32 [64, 64, 4096], P('depth', 'lat')
- surface_new: float32 [64, 4096], P('lat', 'depth')
The draws below stay inside these ranges and needn't reach their ends.
All inputs are finite; a program needn't handle non-finite values. No bound on the sum of `ponded` or of `river` on one device may be relied on, other than what follows from the above.
Results may differ from the reference program's by a relative error of at most 0.0003.
Values sent between devices are 32-bit elements; how exact they have to be, the bound alone decides.
A program may use at most 128 MiB of HBM per device.

```python
import math
import jax
import jax.numpy as jnp

NY = 4096
NSOIL = 12
SWEEPS = 4
NX = 64
NZ = 64


def touch_ends(drawn, rng, low, high):
    spot = [jax.random.randint(jax.random.fold_in(rng, axis), (), 0, length) for axis, length in enumerate(drawn.shape)]
    main_axis = drawn.shape.index(max(drawn.shape))
    neighbour = spot[:main_axis] + [(spot[main_axis] + 1) % drawn.shape[main_axis]] + spot[main_axis + 1:]
    return drawn.at[tuple(spot)].set(low).at[tuple(neighbour)].set(high)


def steps_of(stream_key, dims, cuts, smallest, top_value):
    def one(position, parts):
        draws = jax.random.uniform(jax.random.fold_in(jax.random.fold_in(stream_key, 6), position), (parts,), jnp.float32, smallest / len(cuts), top_value / len(cuts))
        return jnp.repeat(jnp.exp(draws), dims[position] // parts).reshape((-1,) + (1,) * (len(dims) - position - 1))

    gain = one(*cuts[0])
    for cut in cuts[1:]:
        gain = gain * one(*cut)
    return gain


def scatter_about(own_key, shape, deviation, bound, shards=(), held_as=jnp.bfloat16):
    drawn = jax.random.normal(own_key, shape, jnp.float32) * deviation
    if len(shards) > 0:
        drawn = steps_of(own_key, shape, shards, -0.22, 0.18) * drawn
    return jnp.clip(drawn, min=-bound, max=bound).astype(held_as)


def setup_inputs(seed: int = 0) -> dict:
    key_of = jax.random.split(jax.random.key(seed), 11)
    return {
        "head": jnp.clip(-1.0 + 1.5 * jax.random.uniform(key_of[0], (NZ, NX, NY), jnp.float32) ** steps_of(key_of[0], (NZ, NX, NY), ((0, 4), (1, 8)), -0.2, 0.2), -1.0, 0.5),
        "head_old": jnp.clip(-1.0 + 1.5 * jax.random.uniform(key_of[1], (NZ, NX, NY), jnp.float32) ** steps_of(key_of[1], (NZ, NX, NY), ((0, 4), (1, 8)), -0.2, 0.2), -1.0, 0.5),
        "soil": touch_ends(jax.random.randint(key_of[2], (NZ, NX, NY), 0, NSOIL), jax.random.fold_in(key_of[2], 1), 0, NSOIL - 1).astype(jnp.int32),
        "cond_table": jnp.clip(jnp.exp(jax.random.uniform(key_of[3], (NSOIL,), jnp.float32, math.log(0.3), math.log(2.0))), 0.3, 2.0),
        "shape_table": jnp.clip(jnp.exp(jax.random.uniform(key_of[4], (NSOIL,), jnp.float32, math.log(0.3), math.log(1.5))), 0.3, 1.5),
        "pore_table": jnp.clip(jax.random.uniform(key_of[5], (NSOIL,), jnp.float32, 0.2, 0.5), 0.2, 0.5),
        "pond": jnp.clip(0.02 + 0.58000002 * jax.random.uniform(key_of[6], (NX, NY), jnp.float32) ** steps_of(key_of[6], (NX, NY), ((0, 8),), -0.2, 0.2), 0.02, 0.6),
        "ground": scatter_about(key_of[7], (NX, NY), 0.3, 1.5, ((0, 8),), jnp.float32),
        "ponded": touch_ends((jax.random.randint(key_of[8], (NX, NY), 0, 2) < 1).astype(jnp.int32), jax.random.fold_in(key_of[8], 1), 0, 1),
        "river": touch_ends((jax.random.randint(key_of[9], (NX, NY), 0, 8) < 1).astype(jnp.int32), jax.random.fold_in(key_of[9], 1), 0, 1),
    }


TIME_STEP = 20.0
SURFACE_STEP = 2.0
SPECIFIC_STORAGE = 0.01
LAND_CONVEYANCE = 3.0
RIVER_CONVEYANCE = 10.0
SLOPE_FLOOR = 0.01

def lookup(soil, table):
    value = jnp.zeros(soil.shape, jnp.float32)
    for soil_kind in range(table.shape[0]):
        value = jnp.where(soil == soil_kind, table[soil_kind], value)
    return value

def harmonic(first, second):
    total = first + second
    return 2.0 * first * second / jnp.where(total > 0.0, total, 1.0)

def soil_state(head, head_old, soil, cond_table, shape_table, pore_table):
    saturated = lookup(soil, cond_table)
    steepness = lookup(soil, shape_table)
    porosity = lookup(soil, pore_table)
    wetness = jnp.exp(steepness * jnp.minimum(head, 0.0))
    wetness_old = jnp.exp(steepness * jnp.minimum(head_old, 0.0))
    conductivity = saturated * wetness
    storage_change = porosity * (wetness - wetness_old) + SPECIFIC_STORAGE * (head - head_old)
    capacity = SPECIFIC_STORAGE + porosity * steepness * wetness
    return (conductivity, storage_change, capacity)

def vertical_terms(cond_ext, head_ext):
    vface = harmonic(cond_ext[:-1], cond_ext[1:])
    vflux = vface * (head_ext[:-1] - head_ext[1:] + 1.0)
    return (vface, vflux)

def lateral_inflow(conductivity, head, cond_rows, head_rows):
    face_x = harmonic(cond_rows[:, :-1], cond_rows[:, 1:])
    inflow = face_x[:, 1:] * (head_rows[:, 2:] - head) + face_x[:, :-1] * (head_rows[:, :-2] - head)
    cond_cols = jnp.pad(conductivity, ((0, 0), (0, 0), (1, 1)))
    head_cols = jnp.pad(head, ((0, 0), (0, 0), (1, 1)))
    face_y = harmonic(cond_cols[:, :, :-1], cond_cols[:, :, 1:])
    inflow = inflow + face_y[:, :, 1:] * (head_cols[:, :, 2:] - head)
    return inflow + face_y[:, :, :-1] * (head_cols[:, :, :-2] - head)

def newton_system(storage_change, capacity, vface, vflux, lateral, top_term, top_cond, bottom_term):
    inflow = jnp.concatenate([(vflux[0] + top_term)[None], vflux[1:-1]], 0)
    outflow = jnp.concatenate([vflux[1:-1], (vflux[-1] + bottom_term)[None]], 0)
    residual = storage_change / TIME_STEP - (inflow - outflow) - lateral
    diagonal = capacity / TIME_STEP + vface[:-1] + vface[1:]
    diagonal = jnp.concatenate([(diagonal[0] + 2.0 * top_cond)[None], diagonal[1:]], 0)
    return (residual, diagonal, -vface[:-1], -vface[1:])

def thomas(lower, middle, upper, rhs):
    count = middle.shape[0]
    ratios = []
    partial_values = []
    for row_index in range(count):
        if row_index == 0:
            pivot = middle[0]
            partial_values.append(rhs[0] / pivot)
        else:
            pivot = middle[row_index] - lower[row_index] * ratios[-1]
            partial_values.append((rhs[row_index] - lower[row_index] * partial_values[-1]) / pivot)
        ratios.append(upper[row_index] / pivot)
    result = [partial_values[-1]]
    for row_index in reversed(range(count - 1)):
        result.insert(0, partial_values[row_index] - ratios[row_index] * result[0])
    return jnp.stack(result, 0)

def face_k(pond_one, ground_one, conv_one, pond_two, ground_two, conv_two):
    depth_face = 0.5 * (pond_one + pond_two)
    slope = pond_two + ground_two - (pond_one + ground_one)
    return jnp.power(depth_face, 5.0 / 3.0) * harmonic(conv_one, conv_two) / jnp.sqrt(jnp.abs(slope) + SLOPE_FLOOR)

def row_terms(pond, ground, conv, exfil, pond_up, ground_up, conv_up, pond_down, ground_down, conv_down):
    k_up = face_k(pond, ground, conv, pond_up, ground_up, conv_up)
    k_down = face_k(pond, ground, conv, pond_down, ground_down, conv_down)
    k_cols = face_k(pond[:, :-1], ground[:, :-1], conv[:, :-1], pond[:, 1:], ground[:, 1:], conv[:, 1:])
    k_left = jnp.pad(k_cols, ((0, 0), (1, 0)))
    k_right = jnp.pad(k_cols, ((0, 0), (0, 1)))
    ground_left = jnp.pad(ground[:, :-1], ((0, 0), (1, 0)))
    ground_right = jnp.pad(ground[:, 1:], ((0, 0), (0, 1)))
    sdiag = 1.0 / SURFACE_STEP + k_up + k_down + k_left + k_right
    srhs = pond / SURFACE_STEP + exfil + k_up * (ground_up - ground) + k_down * (ground_down - ground)
    srhs = srhs + k_left * (ground_left - ground) + k_right * (ground_right - ground)
    return (k_up, k_down, k_left, k_right, sdiag, srhs)

def sweep(level, level_up, level_down, terms):
    k_up, k_down, k_left, k_right, sdiag, srhs = terms
    left = jnp.pad(level[:, :-1], ((0, 0), (1, 0)))
    right = jnp.pad(level[:, 1:], ((0, 0), (0, 1)))
    return (srhs + k_up * level_up + k_down * level_down + k_left * left + k_right * right) / sdiag

def pad_above(field):
    return jnp.pad(field[:-1], ((1, 0), (0, 0)))

def pad_below(field):
    return jnp.pad(field[1:], ((0, 1), (0, 0)))

def reference(head, head_old, soil, cond_table, shape_table, pore_table, pond, ground, ponded, river):
    conductivity, storage_change, capacity = soil_state(head, head_old, soil, cond_table, shape_table, pore_table)
    zero_layer = jnp.zeros((1,) + head.shape[1:], jnp.float32)
    vface, vflux = vertical_terms(jnp.concatenate([zero_layer, conductivity, zero_layer], 0), jnp.concatenate([zero_layer, head, zero_layer], 0))
    lateral = lateral_inflow(conductivity, head, jnp.pad(conductivity, ((0, 0), (1, 1), (0, 0))), jnp.pad(head, ((0, 0), (1, 1), (0, 0))))
    wet_pond = ponded.astype(jnp.float32) * pond
    top_flux = conductivity[0] * (2.0 * (wet_pond - head[0]) + 1.0)
    residual, diagonal, lower, upper = newton_system(storage_change, capacity, vface, vflux, lateral, top_flux, conductivity[0], conductivity[-1])
    step = thomas(lower, diagonal, upper, -residual)
    head_new = head + step
    exfil = -top_flux
    conveyance = LAND_CONVEYANCE + (RIVER_CONVEYANCE - LAND_CONVEYANCE) * river.astype(jnp.float32)
    terms = row_terms(pond, ground, conveyance, exfil, pad_above(pond), pad_above(ground), pad_above(conveyance), pad_below(pond), pad_below(ground), pad_below(conveyance))
    level = pond
    for sweep_index in range(SWEEPS):
        level = sweep(level, pad_above(level), pad_below(level), terms)
    return (head_new, level)
```

```python
import functools

import jax
import jax.numpy as jnp
from jax import lax
from jax.experimental import pallas as pl
from jax.experimental.pallas import tpu as pltpu
from jax.sharding import PartitionSpec as P

SWEEPS = 4
TIME_STEP = 20.0
SURFACE_STEP = 2.0
SPECIFIC_STORAGE = 0.01
LAND_CONVEYANCE = 3.0
RIVER_CONVEYANCE = 10.0
SLOPE_FLOOR = 0.01
PAD = 128
TINY = 1e-30
MESH = pl.DeviceIdType.MESH


def recip(value):
    guess = pl.reciprocal(value, approx=True)
    return guess * (2.0 - value * guess)


def harmonic(first, second):
    return 2.0 * first * second * recip(jnp.maximum(first + second, TINY))


def lookup(soil, tables):
    masks = [soil == kind for kind in range(1, tables[0].shape[0])]
    found = []
    for table in tables:
        value = jnp.full(soil.shape, table[0], jnp.float32)
        for kind, mask in enumerate(masks):
            value = jnp.where(mask, table[kind + 1], value)
        found.append(value)
    return found


def face_k(depth_face, slope, conveyance):
    power = jnp.exp((5.0 / 3.0) * jnp.log(jnp.maximum(depth_face, TINY)))
    return power * conveyance * lax.rsqrt(jnp.abs(slope) + SLOPE_FLOOR)


def kernel(
    sizes, head, head_old, soil, cond_t, shape_t, pore_t, pond, ground, ponded, river,
    out, surf,
    head_x, cond_x, old_v, soil_v, base_v, capd_v, y_v, r_v, out_v,
    bsend, bsoil, lrecv, flux_v, nsend, m2recv, m3recv, m4send, m4recv,
    top_v, xrecv, pack, srecv, sext, lev_v,
    in_sem, row_sem, out_sem, lat_s, lat_r, m1_s, m1_r, n_s, m2_r, m3_r, m4_s, m4_r,
    x_s, x_r, surf_s, surf_r,
):
    layers, rows, width, lat_count, chunk = sizes
    count = width // chunk
    strip = width // 4
    window = min(strip + 2 * PAD, width)
    lat = lax.axis_index("lat")
    depth = lax.axis_index("depth")
    has_up = lat > 0
    has_down = lat < lat_count - 1
    top_half = depth < 2
    is_top = depth == 0
    outer = (depth == 0) | (depth == 3)
    inner = (depth == 1) | (depth == 2)
    partner = jnp.where(top_half, 1 - depth, 5 - depth)
    middle = 3 - depth
    sign = jnp.where(top_half, 1.0, -1.0).astype(jnp.float32)
    stride = jnp.where(top_half, 1, -1)

    def layer_at(place):
        return jnp.where(top_half, place, layers - 1 - place)

    def start_of(index):
        return jnp.clip(index * strip - PAD, 0, width - window)

    body = pl.ds(PAD, width)
    loads = (
        pltpu.make_async_copy(head, head_x.at[pl.ds(1, layers), :, body], in_sem.at[0]),
        pltpu.make_async_copy(soil, soil_v, in_sem.at[1]),
        pltpu.make_async_copy(head_old, old_v, in_sem.at[2]),
    )
    row_loads = []
    for side, row in ((0, 0), (1, rows - 1)):
        row_loads.append(pltpu.make_async_copy(head.at[:, row, :], bsend.at[side, 0], row_sem.at[side, 0]))
        row_loads.append(pltpu.make_async_copy(soil.at[:, row, :], bsoil.at[side], row_sem.at[side, 1]))
    for copy in row_loads:
        copy.start()
    for copy in loads:
        copy.start()

    barrier = pltpu.get_barrier_semaphore()
    for shift in range(1, 4):
        pl.semaphore_signal(barrier, inc=1, device_id={"depth": lax.rem(depth + shift, 4)}, device_id_type=MESH)

    @pl.when(has_up)
    def _():
        pl.semaphore_signal(barrier, inc=1, device_id={"lat": lat - 1}, device_id_type=MESH)

    @pl.when(has_down)
    def _():
        pl.semaphore_signal(barrier, inc=1, device_id={"lat": lat + 1}, device_id_type=MESH)

    zero_pad = jnp.zeros((layers + 2, rows, PAD), jnp.float32)
    for field in (head_x, cond_x):
        field[:, :, pl.ds(0, PAD)] = zero_pad
        field[:, :, pl.ds(PAD + width, PAD)] = zero_pad

    for side, present in ((0, has_up), (1, has_down)):
        @pl.when(jnp.logical_not(present))
        def _():
            lrecv[side] = jnp.zeros(lrecv.shape[1:], jnp.float32)
            srecv[side] = jnp.zeros(srecv.shape[1:], jnp.float32)

    pl.semaphore_wait(barrier, 3 + jnp.where(has_up, 1, 0) + jnp.where(has_down, 1, 0))

    def lat_copy(side, index):
        cols = pl.ds(pl.multiple_of(index * chunk, 128), chunk)
        return pltpu.make_async_remote_copy(
            src_ref=bsend.at[side, :, :, cols],
            dst_ref=lrecv.at[1 - side, :, :, cols],
            send_sem=lat_s.at[side, index],
            recv_sem=lat_r.at[1 - side, index],
            device_id={"lat": lat - 1 if side == 0 else lat + 1},
            device_id_type=MESH,
        )

    def lat_arrival(side, index):
        cols = pl.ds(pl.multiple_of(index * chunk, 128), chunk)
        return pltpu.make_async_remote_copy(
            src_ref=bsend.at[1 - side, :, :, cols],
            dst_ref=lrecv.at[side, :, :, cols],
            send_sem=lat_s.at[1 - side, index],
            recv_sem=lat_r.at[side, index],
            device_id={"lat": lat - 1 if side == 0 else lat + 1},
            device_id_type=MESH,
        )

    for copy in row_loads:
        copy.wait()

    def boundary(index, carry):
        cols = pl.ds(pl.multiple_of(index * chunk, 128), chunk)
        for side, present in ((0, has_up), (1, has_down)):
            saturated, steep = lookup(bsoil[side, :, cols], (cond_t, shape_t))
            bsend[side, 1, :, cols] = saturated * jnp.exp(steep * jnp.minimum(bsend[side, 0, :, cols], 0.0))

            @pl.when(present)
            def _():
                lat_copy(side, index).start()
        return carry

    lax.fori_loop(0, count, boundary, 0)

    for copy in loads:
        copy.wait()

    def end_layer(layer):
        def step(index, carry):
            cols = pl.ds(pl.multiple_of(index * chunk, 128), chunk)
            wide = pl.ds(pl.multiple_of(index * chunk + PAD, 128), chunk)
            saturated, steep = lookup(soil_v[layer, :, cols], (cond_t, shape_t))
            cond_x[layer + 1, :, wide] = saturated * jnp.exp(steep * jnp.minimum(head_x[layer + 1, :, wide], 0.0))
            return carry
        lax.fori_loop(0, count, step, 0)

    def m1_copy(place, target):
        slot = jnp.where(top_half, layers + 1, 0) if place == 0 else jnp.where(top_half, 0, layers + 1)
        layer = layer_at(0 if place == 0 else layers - 1) + 1
        return [
            pltpu.make_async_remote_copy(
                src_ref=field.at[layer, :, body],
                dst_ref=field.at[slot, :, body],
                send_sem=m1_s.at[place, which],
                recv_sem=m1_r.at[which],
                device_id={"depth": target},
                device_id_type=MESH,
            )
            for which, field in enumerate((head_x, cond_x))
        ]

    def m1_arrival():
        slot = jnp.where(top_half, layers + 1, 0)
        layer = layer_at(layers - 1) + 1
        return [
            pltpu.make_async_remote_copy(
                src_ref=field.at[layer, :, body],
                dst_ref=field.at[slot, :, body],
                send_sem=m1_s.at[1, which],
                recv_sem=m1_r.at[which],
                device_id={"depth": partner},
                device_id_type=MESH,
            )
            for which, field in enumerate((head_x, cond_x))
        ]

    @pl.when(inner)
    def _():
        end_layer(layer_at(layers - 1))
        for copy in m1_copy(1, middle):
            copy.start()
        end_layer(layer_at(0))
        for copy in m1_copy(0, partner):
            copy.start()

    def x_copy(target):
        return pltpu.make_async_remote_copy(
            src_ref=top_v.at[:, pl.ds(min(max(target * strip - PAD, 0), width - window), window)],
            dst_ref=xrecv,
            send_sem=x_s.at[target],
            recv_sem=x_r,
            device_id={"depth": target},
            device_id_type=MESH,
        )

    @pl.when(is_top)
    def _():
        end_layer(0)
        wet = ponded[...].astype(jnp.float32) * pond[...]
        top_v[...] = cond_x[1, :, body] * (2.0 * (wet - head_x[1, :, body]) + 1.0)
        for target in range(1, 4):
            x_copy(target).start()
        xrecv[...] = top_v[:, pl.ds(0, window)]

    def state(index, carry):
        layer = index // count
        begin = lax.rem(index, count) * chunk
        cols = pl.ds(pl.multiple_of(begin, 128), chunk)
        wide = pl.ds(pl.multiple_of(begin + PAD, 128), chunk)
        saturated, steep, pore = lookup(soil_v[layer, :, cols], (cond_t, shape_t, pore_t))
        now = head_x[layer + 1, :, wide]
        old = old_v[layer, :, cols]
        wet = jnp.exp(steep * jnp.minimum(now, 0.0))
        wet_old = jnp.exp(steep * jnp.minimum(old, 0.0))
        value = saturated * wet

        already = (inner & ((layer == 0) | (layer == layers - 1))) | (is_top & (layer == 0))

        @pl.when(jnp.logical_not(already))
        def _():
            cond_x[layer + 1, :, wide] = value

        base_v[layer, :, cols] = (pore * (wet - wet_old) + SPECIFIC_STORAGE * (now - old)) * (1.0 / TIME_STEP)
        capd_v[layer, :, cols] = (SPECIFIC_STORAGE + pore * steep * wet) * (1.0 / TIME_STEP)
        return carry

    lax.fori_loop(0, layers * count, state, 0)

    @pl.when(jnp.logical_not(is_top))
    def _():
        x_copy(1).wait_recv()

    begin = pl.multiple_of(start_of(depth), 128)
    view = pl.ds(begin, window)
    conveyance = LAND_CONVEYANCE + (RIVER_CONVEYANCE - LAND_CONVEYANCE) * river[:, view].astype(jnp.float32)
    own = (pond[:, view], ground[:, view], conveyance, -xrecv[...])
    for place, value in enumerate(own):
        for side, first in ((0, 0), (1, rows - 4)):
            pack[side, pl.ds(4 * place, 4), :] = value[first:first + 4]
        sext[place, pl.ds(4, rows), :] = value

    def surf_copy(side):
        return pltpu.make_async_remote_copy(
            src_ref=pack.at[side],
            dst_ref=srecv.at[1 - side],
            send_sem=surf_s.at[side],
            recv_sem=surf_r.at[1 - side],
            device_id={"lat": lat - 1 if side == 0 else lat + 1},
            device_id_type=MESH,
        )

    def surf_arrival(side):
        return pltpu.make_async_remote_copy(
            src_ref=pack.at[1 - side],
            dst_ref=srecv.at[side],
            send_sem=surf_s.at[1 - side],
            recv_sem=surf_r.at[side],
            device_id={"lat": lat - 1 if side == 0 else lat + 1},
            device_id_type=MESH,
        )

    for side, present in ((0, has_up), (1, has_down)):
        @pl.when(present)
        def _():
            surf_copy(side).start()

    def surface():
        for side, present in ((0, has_up), (1, has_down)):
            @pl.when(present)
            def _():
                surf_arrival(side).wait_recv()
        for place in range(4):
            sext[place, pl.ds(0, 4), :] = srecv[0, pl.ds(4 * place, 4), :]
            sext[place, pl.ds(4 + rows, 4), :] = srecv[1, pl.ds(4 * place, 4), :]
        tall = rows + 8
        depth_w, ground_w, conv_w, exfil = (sext[place] for place in range(4))
        row = lax.broadcasted_iota(jnp.int32, (tall, window), 0)
        col = lax.broadcasted_iota(jnp.int32, (tall, window), 1)

        def after(value, axis):
            return pltpu.roll(value, value.shape[axis] - 1, axis)

        def before(value, axis):
            return pltpu.roll(value, 1, axis)

        total = jnp.full((tall, window), 1.0 / SURFACE_STEP, jnp.float32)
        rhs = depth_w * (1.0 / SURFACE_STEP) + exfil
        faces = []
        for axis, last in ((0, row == tall - 1), (1, col == window - 1)):
            depth_n, ground_n, conv_n = (after(value, axis) for value in (depth_w, ground_w, conv_w))
            k = face_k(
                0.5 * (depth_w + depth_n),
                depth_n + ground_n - (depth_w + ground_w),
                harmonic(conv_w, conv_n),
            )
            k = jnp.where(last, 0.0, k)
            k_before = before(k, axis)
            flow = k * (ground_n - ground_w)
            total = total + k + k_before
            rhs = rhs + flow - before(flow, axis)
            faces.append((axis, k, k_before))
        scale = recip(total)
        level = depth_w
        for _ in range(SWEEPS):
            fed = rhs
            for axis, k, k_before in faces:
                fed = fed + k * after(level, axis) + k_before * before(level, axis)
            level = fed * scale
        lev_v[...] = level[4:4 + rows]
        offset = pl.multiple_of(depth * strip - begin, 128)
        surf[...] = lev_v[:, pl.ds(offset, strip)]

    def m2_copy(index):
        cols = pl.ds(pl.multiple_of(index * chunk, 128), chunk)
        return pltpu.make_async_remote_copy(
            src_ref=nsend.at[:, :, cols], dst_ref=m2recv.at[:, :, cols],
            send_sem=n_s.at[index], recv_sem=m2_r.at[index],
            device_id={"depth": partner}, device_id_type=MESH,
        )

    def m3_copy(index):
        cols = pl.ds(pl.multiple_of(index * chunk, 128), chunk)
        return pltpu.make_async_remote_copy(
            src_ref=nsend.at[:, :, cols], dst_ref=m3recv.at[:, :, cols],
            send_sem=n_s.at[index], recv_sem=m3_r.at[index],
            device_id={"depth": middle}, device_id_type=MESH,
        )

    def m4_copy(index):
        cols = pl.ds(pl.multiple_of(index * chunk, 128), chunk)
        return pltpu.make_async_remote_copy(
            src_ref=m4send.at[:, cols], dst_ref=m4recv.at[:, cols],
            send_sem=m4_s.at[index], recv_sem=m4_r.at[index],
            device_id={"depth": partner}, device_id_type=MESH,
        )

    def out_copy(index):
        cols = pl.ds(pl.multiple_of(index * chunk, 128), chunk)
        return pltpu.make_async_copy(out_v.at[:, :, cols], out.at[:, :, cols], out_sem.at[index])

    for copy in m1_arrival():
        copy.wait_recv()

    row8 = lax.broadcasted_iota(jnp.int32, (rows, chunk), 0)

    def eliminate(index):
        cols = pl.ds(pl.multiple_of(index * chunk, 128), chunk)
        mid = pl.ds(pl.multiple_of(index * chunk + PAD, 128), chunk)
        wide = pl.ds(pl.multiple_of(index * chunk, 128), chunk + 2 * PAD)
        for side, present in ((0, has_up), (1, has_down)):
            @pl.when(present)
            def _():
                lat_arrival(side, index).wait_recv()
            mine_h, mine_c = bsend[side, 0, :, cols], bsend[side, 1, :, cols]
            theirs_h, theirs_c = lrecv[side, 0, :, cols], lrecv[side, 1, :, cols]
            flux_v[side] = harmonic(mine_c, theirs_c) * (theirs_h - mine_h)

        @pl.when(outer)
        def _():
            layer = layer_at(0) + 1
            first = cond_x[layer, :, mid]
            wet = ponded[:, cols].astype(jnp.float32) * pond[:, cols]
            inflow = first * (2.0 * (wet - head_x[layer, :, mid]) + 1.0)
            m2recv[0, :, cols] = jnp.where(is_top, 2.0 * first, 0.0)
            m2recv[1, :, cols] = jnp.where(is_top, inflow, -first)

        @pl.when(inner)
        def _():
            m2_copy(index).wait_recv()

        def step(place, carry):
            extra, inflow = carry
            layer = layer_at(place)
            slot = layer + 1
            cond_w = cond_x[slot, :, wide]
            head_w = head_x[slot, :, wide]
            cond = cond_w[:, PAD:PAD + chunk]
            here = head_w[:, PAD:PAD + chunk]
            face = harmonic(cond, cond_x[slot + stride, :, mid])
            flux = face * (here - head_x[slot + stride, :, mid] + sign)
            size = chunk + 2 * PAD
            cond_a = pltpu.roll(cond_w, size - 1, 1)[:, :chunk + PAD]
            head_a = pltpu.roll(head_w, size - 1, 1)[:, :chunk + PAD]
            along = harmonic(cond_w[:, :chunk + PAD], cond_a) * (head_a - head_w[:, :chunk + PAD])
            lateral = along[:, PAD:] - pltpu.roll(along, 1, 1)[:, PAD:]
            across = harmonic(cond, pltpu.roll(cond, rows - 1, 0)) * (pltpu.roll(here, rows - 1, 0) - here)
            across = jnp.where(row8 == rows - 1, 0.0, across)
            lateral = lateral + across - pltpu.roll(across, 1, 0)
            above = flux_v[0, pl.ds(layer, 1), :]
            below = flux_v[1, pl.ds(layer, 1), :]
            lateral = lateral + jnp.where(row8 == 0, above, jnp.where(row8 == rows - 1, below, 0.0))
            scale = recip(capd_v[layer, :, cols] + face + extra)
            ratio = face * scale
            value = (inflow - flux - base_v[layer, :, cols] + lateral) * scale
            y_v[place, :, cols] = value
            r_v[place, :, cols] = ratio
            return (face - face * ratio, flux + face * value)

        extra, inflow = lax.fori_loop(0, layers, step, (m2recv[0, :, cols], m2recv[1, :, cols]))
        nsend[0, :, cols] = jnp.where(outer, extra, y_v[layers - 1, :, cols])
        nsend[1, :, cols] = jnp.where(outer, inflow, r_v[layers - 1, :, cols])

        @pl.when(outer)
        def _():
            m2_copy(index).start()

        @pl.when(inner)
        def _():
            m3_copy(index).start()

    def substitute(index, beyond):
        cols = pl.ds(pl.multiple_of(index * chunk, 128), chunk)
        mid = pl.ds(pl.multiple_of(index * chunk + PAD, 128), chunk)

        def step(place, found):
            place = layers - 1 - place
            layer = layer_at(place)
            found = y_v[place, :, cols] + r_v[place, :, cols] * found
            out_v[layer, :, cols] = head_x[layer + 1, :, mid] + found
            return found

        found = lax.fori_loop(0, layers, step, beyond)
        out_copy(index).start()
        return found

    def finish_inner(index):
        cols = pl.ds(pl.multiple_of(index * chunk, 128), chunk)
        m3_copy(index).wait_recv()
        y_own, r_own = nsend[0, :, cols], nsend[1, :, cols]
        y_far, r_far = m3recv[0, :, cols], m3recv[1, :, cols]
        m4send[:, cols] = substitute(index, (y_far + r_far * y_own) * recip(1.0 - r_own * r_far))
        m4_copy(index).start()

    def finish_outer(index):
        cols = pl.ds(pl.multiple_of(index * chunk, 128), chunk)
        m4_copy(index).wait_recv()
        substitute(index, m4recv[:, cols])

    def turn(index, carry):
        @pl.when(index < count)
        def _():
            eliminate(index)

        @pl.when(index == count)
        def _():
            surface()

        @pl.when(inner & (index >= 1) & (index <= count))
        def _():
            finish_inner(index - 1)

        @pl.when(outer & (index >= 2))
        def _():
            finish_outer(index - 2)

        return carry

    lax.fori_loop(0, count + 2, turn, 0)

    def drain(index, carry):
        for side, present in ((0, has_up), (1, has_down)):
            @pl.when(present)
            def _():
                lat_copy(side, index).wait_send()

        @pl.when(outer)
        def _():
            m2_copy(index).wait_send()

        @pl.when(inner)
        def _():
            m3_copy(index).wait_send()
            m4_copy(index).wait_send()

        out_copy(index).wait()
        return carry

    lax.fori_loop(0, count, drain, 0)
    for side, present in ((0, has_up), (1, has_down)):
        @pl.when(present)
        def _():
            surf_copy(side).wait_send()

    @pl.when(inner)
    def _():
        for copy in m1_copy(1, middle) + m1_copy(0, partner):
            copy.wait_send()

    @pl.when(is_top)
    def _():
        for target in range(1, 4):
            x_copy(target).wait_send()


def per_device(lat_count, chunk, head, head_old, soil, cond_t, shape_t, pore_t, pond, ground, ponded, river):
    layers, rows, width = head.shape
    chunk = min(chunk, width)
    count = width // chunk
    strip = width // 4
    window = min(strip + 2 * PAD, width)
    f32 = jnp.float32
    padded = (layers + 2, rows, width + 2 * PAD)
    full = (layers, rows, width)
    plane = (rows, width)
    pair = (2, rows, width)
    any_spec = pl.BlockSpec(memory_space=pl.ANY)
    smem = pl.BlockSpec(memory_space=pltpu.SMEM)
    vmem = pl.BlockSpec(memory_space=pltpu.VMEM)
    dma = pltpu.SemaphoreType.DMA
    return pl.pallas_call(
        functools.partial(kernel, (layers, rows, width, lat_count, chunk)),
        out_shape=(jax.ShapeDtypeStruct(full, f32), jax.ShapeDtypeStruct((rows, strip), f32)),
        in_specs=[any_spec] * 3 + [smem] * 3 + [vmem] * 4,
        out_specs=(any_spec, vmem),
        scratch_shapes=[
            pltpu.VMEM(padded, f32),
            pltpu.VMEM(padded, f32),
            pltpu.VMEM(full, f32),
            pltpu.VMEM(full, jnp.int32),
            pltpu.VMEM(full, f32),
            pltpu.VMEM(full, f32),
            pltpu.VMEM(full, f32),
            pltpu.VMEM(full, f32),
            pltpu.VMEM(full, f32),
            pltpu.VMEM((2, 2, layers, width), f32),
            pltpu.VMEM((2, layers, width), jnp.int32),
            pltpu.VMEM((2, 2, layers, width), f32),
            pltpu.VMEM((2, layers, chunk), f32),
            pltpu.VMEM(pair, f32),
            pltpu.VMEM(pair, f32),
            pltpu.VMEM(pair, f32),
            pltpu.VMEM(plane, f32),
            pltpu.VMEM(plane, f32),
            pltpu.VMEM(plane, f32),
            pltpu.VMEM((rows, window), f32),
            pltpu.VMEM((2, 16, window), f32),
            pltpu.VMEM((2, 16, window), f32),
            pltpu.VMEM((4, rows + 8, window), f32),
            pltpu.VMEM((rows, window), f32),
            dma((3,)),
            dma((2, 2)),
            dma((count,)),
            dma((2, count)),
            dma((2, count)),
            dma((2, 2)),
            dma((2,)),
            dma((count,)),
            dma((count,)),
            dma((count,)),
            dma((count,)),
            dma((count,)),
            dma((4,)),
            dma(()),
            dma((2,)),
            dma((2,)),
        ],
        compiler_params=pltpu.CompilerParams(
            collective_id=0, has_side_effects=True, vmem_limit_bytes=56 * 1024 * 1024
        ),
    )(head, head_old, soil, cond_t, shape_t, pore_t, pond, ground, ponded, river)


def solution(mesh):
    deep = P("depth", "lat", None)
    flat = P("lat", None)
    return jax.shard_map(
        functools.partial(per_device, mesh.shape["lat"], 512),
        mesh=mesh,
        in_specs=(deep, deep, deep, P(), P(), P(), flat, flat, flat, flat),
        out_specs=(deep, P("lat", "depth")),
        check_vma=False,
    )
```

```python
import functools

import jax
import jax.numpy as jnp
from jax import lax
from jax.experimental import pallas as pl
from jax.experimental.pallas import tpu as pltpu
from jax.sharding import PartitionSpec as P

SWEEPS = 4
TIME_STEP = 20.0
SURFACE_STEP = 2.0
SPECIFIC_STORAGE = 0.01
LAND_CONVEYANCE = 3.0
RIVER_CONVEYANCE = 10.0
SLOPE_FLOOR = 0.01
PAD = 128
TINY = 1e-30
CLOSED = 3e38
MESH = pl.DeviceIdType.MESH


def recip(value):
    guess = pl.reciprocal(value, approx=True)
    return guess * (2.0 - value * guess)


def harmonic(first, second):
    return 2.0 * first * second * recip(jnp.maximum(first + second, TINY))


def lane_table(table, scale):
    lane = lax.broadcasted_iota(jnp.int32, (8, 128), 1)
    value = jnp.zeros((8, 128), jnp.float32)
    for kind in range(table.shape[0]):
        value = jnp.where(lane == kind, scale * table[kind], value)
    return value


def lookup(soil, table):
    lines = []
    for top in range(0, soil.shape[0], 8):
        tiles = [
            jnp.take_along_axis(
                table, soil[top:top + 8, left:left + 128], axis=1, mode="promise_in_bounds"
            )
            for left in range(0, soil.shape[1], 128)
        ]
        lines.append(jnp.concatenate(tiles, axis=1))
    return lines[0] if len(lines) == 1 else jnp.concatenate(lines, axis=0)


def series(first, second):
    return recip(first + second)


def face_k(depth_face, slope, conveyance):
    power = jnp.exp((5.0 / 3.0) * jnp.log(jnp.maximum(depth_face, TINY)))
    return power * conveyance * lax.rsqrt(jnp.abs(slope) + SLOPE_FLOOR)


def kernel(
    sizes, head, head_old, soil, cond_t, shape_t, pore_t, pond, ground, ponded, river,
    out_v, surf,
    head_x, cond_x, old_v, soil_v, base_v, capd_v, face_v, rhs_v, sum_v, last_v, y_v, r_v,
    bsend, lrecv, flux_v, nsend, m2recv, m3recv, m4send, m4recv,
    top_v, xrecv, pack, srecv, sext, lev_v,
    in_sem, lat_s, lat_r, m1_s, m1_r, n_s, m2_r, m3_r, m4_s, m4_r,
    x_s, x_r, surf_s, surf_r,
):
    layers, rows, width, lat_count, chunk = sizes
    count = width // chunk
    strip = width // 4
    window = min(strip + 2 * PAD, width)
    lat = lax.axis_index("lat")
    depth = lax.axis_index("depth")
    has_up = lat > 0
    has_down = lat < lat_count - 1
    top_half = depth < 2
    is_top = depth == 0
    outer = (depth == 0) | (depth == 3)
    inner = (depth == 1) | (depth == 2)
    partner = jnp.where(top_half, 1 - depth, 5 - depth)
    middle = 3 - depth
    sign = jnp.where(top_half, 1.0, -1.0).astype(jnp.float32)
    stride = jnp.where(top_half, 1, -1)

    def layer_at(place):
        return jnp.where(top_half, place, layers - 1 - place)

    def start_of(index):
        return jnp.clip(index * strip - PAD, 0, width - window)

    body = pl.ds(PAD, width)
    def loads(part):
        cols = pl.ds(pl.multiple_of(part * chunk, 128), chunk)
        wide = pl.ds(pl.multiple_of(part * chunk + PAD, 128), chunk)
        return (
            pltpu.make_async_copy(head.at[:, :, cols], head_x.at[pl.ds(1, layers), :, wide], in_sem.at[0, part]),
            pltpu.make_async_copy(soil.at[:, :, cols], soil_v.at[:, :, cols], in_sem.at[1, part]),
            pltpu.make_async_copy(head_old.at[:, :, cols], old_v.at[:, :, cols], in_sem.at[2, part]),
        )

    def begin_loads(part, carry):
        for copy in loads(part):
            copy.start()
        return carry

    lax.fori_loop(0, count, begin_loads, 0)

    barrier = pltpu.get_barrier_semaphore()
    for shift in range(1, 4):
        pl.semaphore_signal(barrier, inc=1, device_id={"depth": lax.rem(depth + shift, 4)}, device_id_type=MESH)

    @pl.when(has_up)
    def _():
        pl.semaphore_signal(barrier, inc=1, device_id={"lat": lat - 1}, device_id_type=MESH)

    @pl.when(has_down)
    def _():
        pl.semaphore_signal(barrier, inc=1, device_id={"lat": lat + 1}, device_id_type=MESH)

    for field, value in ((head_x, 0.0), (cond_x, CLOSED)):
        filled = jnp.full((layers + 2, rows, PAD), value, jnp.float32)
        field[:, :, pl.ds(0, PAD)] = filled
        field[:, :, pl.ds(PAD + width, PAD)] = filled

    for side, present in ((0, has_up), (1, has_down)):
        @pl.when(jnp.logical_not(present))
        def _():
            lrecv[side, 0] = jnp.zeros(lrecv.shape[2:], jnp.float32)
            lrecv[side, 1] = jnp.full(lrecv.shape[2:], CLOSED, jnp.float32)
            srecv[side] = jnp.zeros(srecv.shape[1:], jnp.float32)

    pl.semaphore_wait(barrier, 3 + jnp.where(has_up, 1, 0) + jnp.where(has_down, 1, 0))

    def lat_copy(side, index):
        cols = pl.ds(pl.multiple_of(index * chunk, 128), chunk)
        return pltpu.make_async_remote_copy(
            src_ref=bsend.at[side, :, :, cols],
            dst_ref=lrecv.at[1 - side, :, :, cols],
            send_sem=lat_s.at[side, index],
            recv_sem=lat_r.at[1 - side, index],
            device_id={"lat": lat - 1 if side == 0 else lat + 1},
            device_id_type=MESH,
        )

    def lat_arrival(side, index):
        cols = pl.ds(pl.multiple_of(index * chunk, 128), chunk)
        return pltpu.make_async_remote_copy(
            src_ref=bsend.at[1 - side, :, :, cols],
            dst_ref=lrecv.at[side, :, :, cols],
            send_sem=lat_s.at[1 - side, index],
            recv_sem=lat_r.at[side, index],
            device_id={"lat": lat - 1 if side == 0 else lat + 1},
            device_id_type=MESH,
        )

    cond_l = lane_table(cond_t, 2.0)
    shape_l = lane_table(shape_t, 1.0)
    pore_l = lane_table(pore_t, 1.0)

    def states(part, carry):
        for copy in loads(part):
            copy.wait()
        cols = pl.ds(pl.multiple_of(part * chunk, 128), chunk)
        wide = pl.ds(pl.multiple_of(part * chunk + PAD, 128), chunk)

        def state(layer, passed):
            kinds = soil_v[layer, :, cols]
            steep, pore = lookup(kinds, shape_l), lookup(kinds, pore_l)
            now = head_x[layer + 1, :, wide]
            old = old_v[layer, :, cols]
            wet = jnp.exp(steep * jnp.minimum(now, 0.0))
            wet_old = jnp.exp(steep * jnp.minimum(old, 0.0))
            inverse = recip(lookup(kinds, cond_l) * wet)
            cond_x[layer + 1, :, wide] = inverse
            for side, row in ((0, 0), (1, rows - 1)):
                bsend[side, 0, pl.ds(layer, 1), cols] = now[row:row + 1]
                bsend[side, 1, pl.ds(layer, 1), cols] = inverse[row:row + 1]
            change = pore * (wet - wet_old) + SPECIFIC_STORAGE * (now - old)
            base_v[layer, :, cols] = change * (1.0 / TIME_STEP)
            capd_v[layer, :, cols] = (SPECIFIC_STORAGE + pore * steep * wet) * (1.0 / TIME_STEP)
            return passed

        lax.fori_loop(0, layers, state, 0, unroll=4)
        for side, present in ((0, has_up), (1, has_down)):
            @pl.when(present)
            def _():
                lat_copy(side, part).start()
        return carry

    lax.fori_loop(0, count, states, 0)

    def m1_copy(place, target):
        slot = jnp.where(top_half, layers + 1, 0) if place == 0 else jnp.where(top_half, 0, layers + 1)
        layer = layer_at(0 if place == 0 else layers - 1) + 1
        return [
            pltpu.make_async_remote_copy(
                src_ref=field.at[layer, :, body],
                dst_ref=field.at[slot, :, body],
                send_sem=m1_s.at[place, which],
                recv_sem=m1_r.at[which],
                device_id={"depth": target},
                device_id_type=MESH,
            )
            for which, field in enumerate((head_x, cond_x))
        ]

    def m1_arrival():
        slot = jnp.where(top_half, layers + 1, 0)
        layer = layer_at(layers - 1) + 1
        return [
            pltpu.make_async_remote_copy(
                src_ref=field.at[layer, :, body],
                dst_ref=field.at[slot, :, body],
                send_sem=m1_s.at[1, which],
                recv_sem=m1_r.at[which],
                device_id={"depth": partner},
                device_id_type=MESH,
            )
            for which, field in enumerate((head_x, cond_x))
        ]

    @pl.when(inner)
    def _():
        for copy in m1_copy(1, middle):
            copy.start()
        for copy in m1_copy(0, partner):
            copy.start()

    def x_copy(target):
        return pltpu.make_async_remote_copy(
            src_ref=top_v.at[:, pl.ds(min(max(target * strip - PAD, 0), width - window), window)],
            dst_ref=xrecv,
            send_sem=x_s.at[target],
            recv_sem=x_r,
            device_id={"depth": target},
            device_id_type=MESH,
        )

    @pl.when(is_top)
    def _():
        wet = ponded[...].astype(jnp.float32) * pond[...]
        top_v[...] = 0.5 * recip(cond_x[1, :, body]) * (2.0 * (wet - head_x[1, :, body]) + 1.0)
        for target in range(1, 4):
            x_copy(target).start()
        xrecv[...] = top_v[:, pl.ds(0, window)]

    @pl.when(jnp.logical_not(is_top))
    def _():
        x_copy(1).wait_recv()

    begin = pl.multiple_of(start_of(depth), 128)
    view = pl.ds(begin, window)
    conveyance = LAND_CONVEYANCE + (RIVER_CONVEYANCE - LAND_CONVEYANCE) * river[:, view].astype(jnp.float32)
    own = (pond[:, view], ground[:, view], conveyance, -xrecv[...])
    for place, value in enumerate(own):
        for side, first in ((0, 0), (1, rows - 4)):
            pack[side, pl.ds(4 * place, 4), :] = value[first:first + 4]
        sext[place, pl.ds(4, rows), :] = value

    def surf_copy(side):
        return pltpu.make_async_remote_copy(
            src_ref=pack.at[side],
            dst_ref=srecv.at[1 - side],
            send_sem=surf_s.at[side],
            recv_sem=surf_r.at[1 - side],
            device_id={"lat": lat - 1 if side == 0 else lat + 1},
            device_id_type=MESH,
        )

    def surf_arrival(side):
        return pltpu.make_async_remote_copy(
            src_ref=pack.at[1 - side],
            dst_ref=srecv.at[side],
            send_sem=surf_s.at[1 - side],
            recv_sem=surf_r.at[side],
            device_id={"lat": lat - 1 if side == 0 else lat + 1},
            device_id_type=MESH,
        )

    for side, present in ((0, has_up), (1, has_down)):
        @pl.when(present)
        def _():
            surf_copy(side).start()

    def surface():
        for side, present in ((0, has_up), (1, has_down)):
            @pl.when(present)
            def _():
                surf_arrival(side).wait_recv()
        for place in range(4):
            sext[place, pl.ds(0, 4), :] = srecv[0, pl.ds(4 * place, 4), :]
            sext[place, pl.ds(4 + rows, 4), :] = srecv[1, pl.ds(4 * place, 4), :]
        tall = rows + 8
        depth_w, ground_w, conv_w, exfil = (sext[place] for place in range(4))
        row = lax.broadcasted_iota(jnp.int32, (tall, window), 0)
        col = lax.broadcasted_iota(jnp.int32, (tall, window), 1)

        def after(value, axis):
            return pltpu.roll(value, value.shape[axis] - 1, axis)

        def before(value, axis):
            return pltpu.roll(value, 1, axis)

        total = jnp.full((tall, window), 1.0 / SURFACE_STEP, jnp.float32)
        rhs = depth_w * (1.0 / SURFACE_STEP) + exfil
        faces = []
        for axis, last in ((0, row == tall - 1), (1, col == window - 1)):
            depth_n, ground_n, conv_n = (after(value, axis) for value in (depth_w, ground_w, conv_w))
            k = face_k(
                0.5 * (depth_w + depth_n),
                depth_n + ground_n - (depth_w + ground_w),
                harmonic(conv_w, conv_n),
            )
            k = jnp.where(last, 0.0, k)
            k_before = before(k, axis)
            flow = k * (ground_n - ground_w)
            total = total + k + k_before
            rhs = rhs + flow - before(flow, axis)
            faces.append((axis, k, k_before))
        scale = recip(total)
        level = depth_w
        for _ in range(SWEEPS):
            fed = rhs
            for axis, k, k_before in faces:
                fed = fed + k * after(level, axis) + k_before * before(level, axis)
            level = fed * scale
        lev_v[...] = level[4:4 + rows]
        offset = pl.multiple_of(depth * strip - begin, 128)
        surf[...] = lev_v[:, pl.ds(offset, strip)]

    def m2_copy(index):
        cols = pl.ds(pl.multiple_of(index * chunk, 128), chunk)
        return pltpu.make_async_remote_copy(
            src_ref=nsend.at[:, :, cols], dst_ref=m2recv.at[:, :, cols],
            send_sem=n_s.at[index], recv_sem=m2_r.at[index],
            device_id={"depth": partner}, device_id_type=MESH,
        )

    def m3_copy(index):
        cols = pl.ds(pl.multiple_of(index * chunk, 128), chunk)
        return pltpu.make_async_remote_copy(
            src_ref=nsend.at[:, :, cols], dst_ref=m3recv.at[:, :, cols],
            send_sem=n_s.at[index], recv_sem=m3_r.at[index],
            device_id={"depth": middle}, device_id_type=MESH,
        )

    def m4_copy(index):
        cols = pl.ds(pl.multiple_of(index * chunk, 128), chunk)
        return pltpu.make_async_remote_copy(
            src_ref=m4send.at[:, cols], dst_ref=m4recv.at[:, cols],
            send_sem=m4_s.at[index], recv_sem=m4_r.at[index],
            device_id={"depth": partner}, device_id_type=MESH,
        )

    for copy in m1_arrival():
        copy.wait_recv()

    row8 = lax.broadcasted_iota(jnp.int32, (rows, chunk), 0)

    def local_terms(index, outside):
        cols = pl.ds(pl.multiple_of(index * chunk, 128), chunk)
        mid = pl.ds(pl.multiple_of(index * chunk + PAD, 128), chunk)
        wide = pl.ds(pl.multiple_of(index * chunk, 128), chunk + 2 * PAD)
        first_cond = 0.5 * recip(cond_x[layer_at(0) + 1, :, mid])
        wet = ponded[:, cols].astype(jnp.float32) * pond[:, cols]
        top = first_cond * (2.0 * (wet - head_x[layer_at(0) + 1, :, mid]) + 1.0)
        face_0 = jnp.where(is_top, 2.0 * first_cond, 0.0)
        flux_0 = jnp.where(is_top, top, jnp.where(depth == 3, -first_cond, 0.0))
        size = chunk + 2 * PAD
        most = chunk + PAD

        def step(place, carry):
            face_b, flux_b = carry
            layer = layer_at(place)
            slot = layer + 1
            cond_w = cond_x[slot, :, wide]
            head_w = head_x[slot, :, wide]
            cond = cond_w[:, PAD:PAD + chunk]
            here = head_w[:, PAD:PAD + chunk]
            face = series(cond, cond_x[slot + stride, :, mid])
            flux = face * (here - head_x[slot + stride, :, mid] + sign)
            cond_a = pltpu.roll(cond_w, size - 1, 1)[:, :most]
            head_a = pltpu.roll(head_w, size - 1, 1)[:, :most]
            along = series(cond_w[:, :most], cond_a) * (head_a - head_w[:, :most])
            lateral = along[:, PAD:] - pltpu.roll(along, 1, 1)[:, PAD:]
            across = series(cond, pltpu.roll(cond, rows - 1, 0)) * (pltpu.roll(here, rows - 1, 0) - here)
            across = jnp.where(row8 == rows - 1, 0.0, across)
            lateral = lateral + across - pltpu.roll(across, 1, 0)
            face_v[place, :, cols] = face
            sum_v[place, :, cols] = capd_v[layer, :, cols] + face + face_b
            rhs_v[place, :, cols] = flux_b - flux - base_v[layer, :, cols] + lateral
            return (face, flux)

        face, flux = lax.fori_loop(0, layers, step, (face_0, flux_0), unroll=4)
        last_v[:, cols] = flux
        return outside

    lax.fori_loop(0, count, local_terms, 0)

    def eliminate(index):
        cols = pl.ds(pl.multiple_of(index * chunk, 128), chunk)
        for side, present in ((0, has_up), (1, has_down)):
            @pl.when(present)
            def _():
                lat_arrival(side, index).wait_recv()
            mine_h, mine_c = bsend[side, 0, :, cols], bsend[side, 1, :, cols]
            theirs_h, theirs_c = lrecv[side, 0, :, cols], lrecv[side, 1, :, cols]
            flux_v[side] = series(mine_c, theirs_c) * (theirs_h - mine_h)

        @pl.when(outer)
        def _():
            m2recv[0, :, cols] = jnp.zeros((rows, chunk), jnp.float32)
            m2recv[1, :, cols] = jnp.zeros((rows, chunk), jnp.float32)

        @pl.when(inner)
        def _():
            m2_copy(index).wait_recv()

        def step(place, carry):
            extra, inflow = carry
            layer = layer_at(place)
            above = flux_v[0, pl.ds(layer, 1), :]
            below = flux_v[1, pl.ds(layer, 1), :]
            lateral = jnp.where(row8 == 0, above, jnp.where(row8 == rows - 1, below, 0.0))
            face = face_v[place, :, cols]
            scale = recip(sum_v[place, :, cols] + extra)
            ratio = face * scale
            value = (inflow + (rhs_v[place, :, cols] + lateral)) * scale
            y_v[place, :, cols] = value
            r_v[place, :, cols] = ratio
            return (-(face * ratio), face * value)

        extra, inflow = lax.fori_loop(
            0, layers, step, (m2recv[0, :, cols], m2recv[1, :, cols]), unroll=4
        )
        last = layers - 1
        nsend[0, :, cols] = jnp.where(outer, extra + face_v[last, :, cols], y_v[last, :, cols])
        nsend[1, :, cols] = jnp.where(outer, inflow + last_v[:, cols], r_v[last, :, cols])

        @pl.when(outer)
        def _():
            m2_copy(index).start()

        @pl.when(inner)
        def _():
            m3_copy(index).start()

    def substitute(index, beyond):
        cols = pl.ds(pl.multiple_of(index * chunk, 128), chunk)
        mid = pl.ds(pl.multiple_of(index * chunk + PAD, 128), chunk)

        def step(place, found):
            place = layers - 1 - place
            layer = layer_at(place)
            found = y_v[place, :, cols] + r_v[place, :, cols] * found
            out_v[layer, :, cols] = head_x[layer + 1, :, mid] + found
            return found

        found = lax.fori_loop(0, layers, step, beyond, unroll=4)
        return found

    def finish_inner(index):
        cols = pl.ds(pl.multiple_of(index * chunk, 128), chunk)
        m3_copy(index).wait_recv()
        y_own, r_own = nsend[0, :, cols], nsend[1, :, cols]
        y_far, r_far = m3recv[0, :, cols], m3recv[1, :, cols]
        m4send[:, cols] = substitute(index, (y_far + r_far * y_own) * recip(1.0 - r_own * r_far))
        m4_copy(index).start()

    def finish_outer(index):
        cols = pl.ds(pl.multiple_of(index * chunk, 128), chunk)
        m4_copy(index).wait_recv()
        substitute(index, m4recv[:, cols])

    def turn(index, carry):
        @pl.when(index < count)
        def _():
            eliminate(index)

        @pl.when(inner & (index >= 1) & (index <= count))
        def _():
            finish_inner(index - 1)

        @pl.when(index == count + 1)
        def _():
            surface()

        @pl.when(outer & (index >= 2))
        def _():
            finish_outer(index - 2)

        return carry

    lax.fori_loop(0, count + 2, turn, 0)

    def drain(index, carry):
        for side, present in ((0, has_up), (1, has_down)):
            @pl.when(present)
            def _():
                lat_copy(side, index).wait_send()

        @pl.when(outer)
        def _():
            m2_copy(index).wait_send()

        @pl.when(inner)
        def _():
            m3_copy(index).wait_send()
            m4_copy(index).wait_send()

        return carry

    lax.fori_loop(0, count, drain, 0)
    for side, present in ((0, has_up), (1, has_down)):
        @pl.when(present)
        def _():
            surf_copy(side).wait_send()

    @pl.when(inner)
    def _():
        for copy in m1_copy(1, middle) + m1_copy(0, partner):
            copy.wait_send()

    @pl.when(is_top)
    def _():
        for target in range(1, 4):
            x_copy(target).wait_send()


def per_device(lat_count, chunk, head, head_old, soil, cond_t, shape_t, pore_t, pond, ground, ponded, river):
    layers, rows, width = head.shape
    chunk = min(chunk, width)
    count = width // chunk
    strip = width // 4
    window = min(strip + 2 * PAD, width)
    f32 = jnp.float32
    padded = (layers + 2, rows, width + 2 * PAD)
    full = (layers, rows, width)
    plane = (rows, width)
    pair = (2, rows, width)
    any_spec = pl.BlockSpec(memory_space=pl.ANY)
    smem = pl.BlockSpec(memory_space=pltpu.SMEM)
    vmem = pl.BlockSpec(memory_space=pltpu.VMEM)
    dma = pltpu.SemaphoreType.DMA
    return pl.pallas_call(
        functools.partial(kernel, (layers, rows, width, lat_count, chunk)),
        out_shape=(pltpu.VMEM(full, f32), pltpu.VMEM((rows, strip), f32)),
        in_specs=[any_spec] * 3 + [smem] * 3 + [vmem] * 4,
        out_specs=(vmem, vmem),
        scratch_shapes=[
            pltpu.VMEM(padded, f32),
            pltpu.VMEM(padded, f32),
            pltpu.VMEM(full, f32),
            pltpu.VMEM(full, jnp.int32),
            pltpu.VMEM(full, f32),
            pltpu.VMEM(full, f32),
            pltpu.VMEM(full, f32),
            pltpu.VMEM(full, f32),
            pltpu.VMEM(full, f32),
            pltpu.VMEM(plane, f32),
            pltpu.VMEM(full, f32),
            pltpu.VMEM(full, f32),
            pltpu.VMEM((2, 2, layers, width), f32),
            pltpu.VMEM((2, 2, layers, width), f32),
            pltpu.VMEM((2, layers, chunk), f32),
            pltpu.VMEM(pair, f32),
            pltpu.VMEM(pair, f32),
            pltpu.VMEM(pair, f32),
            pltpu.VMEM(plane, f32),
            pltpu.VMEM(plane, f32),
            pltpu.VMEM(plane, f32),
            pltpu.VMEM((rows, window), f32),
            pltpu.VMEM((2, 16, window), f32),
            pltpu.VMEM((2, 16, window), f32),
            pltpu.VMEM((4, rows + 8, window), f32),
            pltpu.VMEM((rows, window), f32),
            dma((3, count)),
            dma((2, count)),
            dma((2, count)),
            dma((2, 2)),
            dma((2,)),
            dma((count,)),
            dma((count,)),
            dma((count,)),
            dma((count,)),
            dma((count,)),
            dma((4,)),
            dma(()),
            dma((2,)),
            dma((2,)),
        ],
        compiler_params=pltpu.CompilerParams(
            collective_id=0, has_side_effects=True, vmem_limit_bytes=61 * 1024 * 1024
        ),
    )(head, head_old, soil, cond_t, shape_t, pore_t, pond, ground, ponded, river)


def solution(mesh):
    deep = P("depth", "lat", None)
    flat = P("lat", None)
    return jax.shard_map(
        functools.partial(per_device, mesh.shape["lat"], 512),
        mesh=mesh,
        in_specs=(deep, deep, deep, P(), P(), P(), flat, flat, flat, flat),
        out_specs=(deep, P("lat", "depth")),
        check_vma=False,
    )
```

```python
import functools

import jax
import jax.numpy as jnp
from jax import lax
from jax.experimental import pallas as pl
from jax.experimental.pallas import tpu as pltpu
from jax.sharding import PartitionSpec as P

SWEEPS = 4
TIME_STEP = 20.0
SURFACE_STEP = 2.0
SPECIFIC_STORAGE = 0.01
LAND_CONVEYANCE = 3.0
RIVER_CONVEYANCE = 10.0
SLOPE_FLOOR = 0.01
PAD = 128
TINY = 1e-30
CLOSED = 3e38
MESH = pl.DeviceIdType.MESH


def recip(value):
    guess = pl.reciprocal(value, approx=True)
    return guess * (2.0 - value * guess)


def harmonic(first, second):
    return 2.0 * first * second * recip(jnp.maximum(first + second, TINY))


def lane_table(table, scale):
    lane = lax.broadcasted_iota(jnp.int32, (8, 128), 1)
    value = jnp.zeros((8, 128), jnp.float32)
    for kind in range(table.shape[0]):
        value = jnp.where(lane == kind, scale * table[kind], value)
    return value


def lookup(soil, table):
    lines = []
    for top in range(0, soil.shape[0], 8):
        tiles = [
            jnp.take_along_axis(
                table, soil[top:top + 8, left:left + 128], axis=1, mode="promise_in_bounds"
            )
            for left in range(0, soil.shape[1], 128)
        ]
        lines.append(jnp.concatenate(tiles, axis=1))
    return lines[0] if len(lines) == 1 else jnp.concatenate(lines, axis=0)


def series(first, second):
    return recip(first + second)


def face_k(depth_face, slope, conveyance):
    power = jnp.exp((5.0 / 3.0) * jnp.log(jnp.maximum(depth_face, TINY)))
    return power * conveyance * lax.rsqrt(jnp.abs(slope) + SLOPE_FLOOR)


def kernel(
    sizes, head, head_old, soil, cond_t, shape_t, pore_t, pond, ground, ponded, river,
    out_v, surf,
    head_x, cond_x, old_v, soil_v, base_v, capd_v, face_v, rhs_v, sum_v, last_v, y_v, r_v,
    bsend, lrecv, flux_v, nsend, m2recv, m3recv, m4send, m4recv,
    top_v, xrecv, pack, srecv, sext, lev_v,
    in_sem, lat_s, lat_r, ans_s, ans_r, m1_s, m1_r, n_s, m2_r, m3_r, m4_s, m4_r,
    x_s, x_r, surf_s, surf_r,
):
    layers, rows, width, lat_count, chunk = sizes
    count = width // chunk
    strip = width // 4
    window = min(strip + 2 * PAD, width)
    lat = lax.axis_index("lat")
    depth = lax.axis_index("depth")
    has_up = lat > 0
    has_down = lat < lat_count - 1
    top_half = depth < 2
    is_top = depth == 0
    outer = (depth == 0) | (depth == 3)
    inner = (depth == 1) | (depth == 2)
    partner = jnp.where(top_half, 1 - depth, 5 - depth)
    middle = 3 - depth
    sign = jnp.where(top_half, 1.0, -1.0).astype(jnp.float32)
    stride = jnp.where(top_half, 1, -1)

    def layer_at(place):
        return jnp.where(top_half, place, layers - 1 - place)

    def start_of(index):
        return jnp.clip(index * strip - PAD, 0, width - window)

    body = pl.ds(PAD, width)
    def loads(part):
        cols = pl.ds(pl.multiple_of(part * chunk, 128), chunk)
        wide = pl.ds(pl.multiple_of(part * chunk + PAD, 128), chunk)
        return (
            pltpu.make_async_copy(head.at[:, :, cols], head_x.at[pl.ds(1, layers), :, wide], in_sem.at[0, part]),
            pltpu.make_async_copy(soil.at[:, :, cols], soil_v.at[:, :, cols], in_sem.at[1, part]),
            pltpu.make_async_copy(head_old.at[:, :, cols], old_v.at[:, :, cols], in_sem.at[2, part]),
        )

    def begin_loads(part, carry):
        for copy in loads(part):
            copy.start()
        return carry

    lax.fori_loop(0, count, begin_loads, 0)

    barrier = pltpu.get_barrier_semaphore()
    for shift in range(1, 4):
        pl.semaphore_signal(barrier, inc=1, device_id={"depth": lax.rem(depth + shift, 4)}, device_id_type=MESH)

    @pl.when(has_up)
    def _():
        pl.semaphore_signal(barrier, inc=1, device_id={"lat": lat - 1}, device_id_type=MESH)

    @pl.when(has_down)
    def _():
        pl.semaphore_signal(barrier, inc=1, device_id={"lat": lat + 1}, device_id_type=MESH)

    for field, value in ((head_x, 0.0), (cond_x, CLOSED)):
        filled = jnp.full((layers + 2, rows, PAD), value, jnp.float32)
        field[:, :, pl.ds(0, PAD)] = filled
        field[:, :, pl.ds(PAD + width, PAD)] = filled

    for side, present in ((0, has_up), (1, has_down)):
        @pl.when(jnp.logical_not(present))
        def _():
            flux_v[side] = jnp.zeros(flux_v.shape[1:], jnp.float32)
            srecv[side] = jnp.zeros(srecv.shape[1:], jnp.float32)

    pl.semaphore_wait(barrier, 3 + jnp.where(has_up, 1, 0) + jnp.where(has_down, 1, 0))

    def neighbour(side):
        return lat - 1 if side == 0 else lat + 1

    def ask_copy(side, index):
        cols = pl.ds(pl.multiple_of(index * chunk, 128), chunk)
        return pltpu.make_async_remote_copy(
            src_ref=bsend.at[side, :, :, cols],
            dst_ref=lrecv.at[:, :, cols],
            send_sem=lat_s.at[index],
            recv_sem=lat_r.at[index],
            device_id={"lat": neighbour(side)},
            device_id_type=MESH,
        )

    def answer_copy(side, index):
        cols = pl.ds(pl.multiple_of(index * chunk, 128), chunk)
        return pltpu.make_async_remote_copy(
            src_ref=flux_v.at[side, :, cols],
            dst_ref=flux_v.at[1 - side, :, cols],
            send_sem=ans_s.at[index],
            recv_sem=ans_r.at[index],
            device_id={"lat": neighbour(side)},
            device_id_type=MESH,
        )

    def answer_arrival(side, index):
        cols = pl.ds(pl.multiple_of(index * chunk, 128), chunk)
        return pltpu.make_async_remote_copy(
            src_ref=flux_v.at[1 - side, :, cols],
            dst_ref=flux_v.at[side, :, cols],
            send_sem=ans_s.at[index],
            recv_sem=ans_r.at[index],
            device_id={"lat": neighbour(side)},
            device_id_type=MESH,
        )

    def by_parity(index):
        odd = lax.rem(index, 2) == 1
        even = jnp.logical_not(odd)
        return ((1, 0, even & has_down, even & has_up), (0, 1, odd & has_up, odd & has_down))

    cond_l = lane_table(cond_t, 2.0)
    shape_l = lane_table(shape_t, 1.0)
    pore_l = lane_table(pore_t, 1.0)

    def states(part, carry):
        for copy in loads(part):
            copy.wait()
        cols = pl.ds(pl.multiple_of(part * chunk, 128), chunk)
        wide = pl.ds(pl.multiple_of(part * chunk + PAD, 128), chunk)

        def state(layer, passed):
            kinds = soil_v[layer, :, cols]
            steep, pore = lookup(kinds, shape_l), lookup(kinds, pore_l)
            now = head_x[layer + 1, :, wide]
            old = old_v[layer, :, cols]
            wet = jnp.exp(steep * jnp.minimum(now, 0.0))
            wet_old = jnp.exp(steep * jnp.minimum(old, 0.0))
            inverse = recip(lookup(kinds, cond_l) * wet)
            cond_x[layer + 1, :, wide] = inverse
            for side, row in ((0, 0), (1, rows - 1)):
                bsend[side, 0, pl.ds(layer, 1), cols] = now[row:row + 1]
                bsend[side, 1, pl.ds(layer, 1), cols] = inverse[row:row + 1]
            change = pore * (wet - wet_old) + SPECIFIC_STORAGE * (now - old)
            base_v[layer, :, cols] = change * (1.0 / TIME_STEP)
            capd_v[layer, :, cols] = (SPECIFIC_STORAGE + pore * steep * wet) * (1.0 / TIME_STEP)
            return passed

        lax.fori_loop(0, layers, state, 0, unroll=4)
        for side, _, asks, _ in by_parity(part):
            @pl.when(asks)
            def _():
                ask_copy(side, part).start()
        return carry

    lax.fori_loop(0, count, states, 0)

    def m1_copy(place, target):
        slot = jnp.where(top_half, layers + 1, 0) if place == 0 else jnp.where(top_half, 0, layers + 1)
        layer = layer_at(0 if place == 0 else layers - 1) + 1
        return [
            pltpu.make_async_remote_copy(
                src_ref=field.at[layer, :, body],
                dst_ref=field.at[slot, :, body],
                send_sem=m1_s.at[place, which],
                recv_sem=m1_r.at[which],
                device_id={"depth": target},
                device_id_type=MESH,
            )
            for which, field in enumerate((head_x, cond_x))
        ]

    def m1_arrival():
        slot = jnp.where(top_half, layers + 1, 0)
        layer = layer_at(layers - 1) + 1
        return [
            pltpu.make_async_remote_copy(
                src_ref=field.at[layer, :, body],
                dst_ref=field.at[slot, :, body],
                send_sem=m1_s.at[1, which],
                recv_sem=m1_r.at[which],
                device_id={"depth": partner},
                device_id_type=MESH,
            )
            for which, field in enumerate((head_x, cond_x))
        ]

    @pl.when(inner)
    def _():
        for copy in m1_copy(1, middle):
            copy.start()
        for copy in m1_copy(0, partner):
            copy.start()

    def x_copy(target):
        return pltpu.make_async_remote_copy(
            src_ref=top_v.at[:, pl.ds(min(max(target * strip - PAD, 0), width - window), window)],
            dst_ref=xrecv,
            send_sem=x_s.at[target],
            recv_sem=x_r,
            device_id={"depth": target},
            device_id_type=MESH,
        )

    @pl.when(is_top)
    def _():
        wet = ponded[...].astype(jnp.float32) * pond[...]
        top_v[...] = 0.5 * recip(cond_x[1, :, body]) * (2.0 * (wet - head_x[1, :, body]) + 1.0)
        for target in range(1, 4):
            x_copy(target).start()
        xrecv[...] = top_v[:, pl.ds(0, window)]

    @pl.when(jnp.logical_not(is_top))
    def _():
        x_copy(1).wait_recv()

    begin = pl.multiple_of(start_of(depth), 128)
    view = pl.ds(begin, window)
    conveyance = LAND_CONVEYANCE + (RIVER_CONVEYANCE - LAND_CONVEYANCE) * river[:, view].astype(jnp.float32)
    own = (pond[:, view], ground[:, view], conveyance, -xrecv[...])
    for place, value in enumerate(own):
        for side, first in ((0, 0), (1, rows - 4)):
            pack[side, pl.ds(4 * place, 4), :] = value[first:first + 4]
        sext[place, pl.ds(4, rows), :] = value

    def surf_copy(side):
        return pltpu.make_async_remote_copy(
            src_ref=pack.at[side],
            dst_ref=srecv.at[1 - side],
            send_sem=surf_s.at[side],
            recv_sem=surf_r.at[1 - side],
            device_id={"lat": lat - 1 if side == 0 else lat + 1},
            device_id_type=MESH,
        )

    def surf_arrival(side):
        return pltpu.make_async_remote_copy(
            src_ref=pack.at[1 - side],
            dst_ref=srecv.at[side],
            send_sem=surf_s.at[1 - side],
            recv_sem=surf_r.at[side],
            device_id={"lat": lat - 1 if side == 0 else lat + 1},
            device_id_type=MESH,
        )

    for side, present in ((0, has_up), (1, has_down)):
        @pl.when(present)
        def _():
            surf_copy(side).start()

    def surface():
        for side, present in ((0, has_up), (1, has_down)):
            @pl.when(present)
            def _():
                surf_arrival(side).wait_recv()
        for place in range(4):
            sext[place, pl.ds(0, 4), :] = srecv[0, pl.ds(4 * place, 4), :]
            sext[place, pl.ds(4 + rows, 4), :] = srecv[1, pl.ds(4 * place, 4), :]
        tall = rows + 8
        depth_w, ground_w, conv_w, exfil = (sext[place] for place in range(4))
        row = lax.broadcasted_iota(jnp.int32, (tall, window), 0)
        col = lax.broadcasted_iota(jnp.int32, (tall, window), 1)

        def after(value, axis):
            return pltpu.roll(value, value.shape[axis] - 1, axis)

        def before(value, axis):
            return pltpu.roll(value, 1, axis)

        total = jnp.full((tall, window), 1.0 / SURFACE_STEP, jnp.float32)
        rhs = depth_w * (1.0 / SURFACE_STEP) + exfil
        faces = []
        for axis, last in ((0, row == tall - 1), (1, col == window - 1)):
            depth_n, ground_n, conv_n = (after(value, axis) for value in (depth_w, ground_w, conv_w))
            k = face_k(
                0.5 * (depth_w + depth_n),
                depth_n + ground_n - (depth_w + ground_w),
                harmonic(conv_w, conv_n),
            )
            k = jnp.where(last, 0.0, k)
            k_before = before(k, axis)
            flow = k * (ground_n - ground_w)
            total = total + k + k_before
            rhs = rhs + flow - before(flow, axis)
            faces.append((axis, k, k_before))
        scale = recip(total)
        level = depth_w
        for _ in range(SWEEPS):
            fed = rhs
            for axis, k, k_before in faces:
                fed = fed + k * after(level, axis) + k_before * before(level, axis)
            level = fed * scale
        lev_v[...] = level[4:4 + rows]
        offset = pl.multiple_of(depth * strip - begin, 128)
        surf[...] = lev_v[:, pl.ds(offset, strip)]

    def m2_copy(index):
        cols = pl.ds(pl.multiple_of(index * chunk, 128), chunk)
        return pltpu.make_async_remote_copy(
            src_ref=nsend.at[:, :, cols], dst_ref=m2recv.at[:, :, cols],
            send_sem=n_s.at[index], recv_sem=m2_r.at[index],
            device_id={"depth": partner}, device_id_type=MESH,
        )

    def m3_copy(index):
        cols = pl.ds(pl.multiple_of(index * chunk, 128), chunk)
        return pltpu.make_async_remote_copy(
            src_ref=nsend.at[:, :, cols], dst_ref=m3recv.at[:, :, cols],
            send_sem=n_s.at[index], recv_sem=m3_r.at[index],
            device_id={"depth": middle}, device_id_type=MESH,
        )

    def m4_copy(index):
        cols = pl.ds(pl.multiple_of(index * chunk, 128), chunk)
        return pltpu.make_async_remote_copy(
            src_ref=m4send.at[:, cols], dst_ref=m4recv.at[:, cols],
            send_sem=m4_s.at[index], recv_sem=m4_r.at[index],
            device_id={"depth": partner}, device_id_type=MESH,
        )

    for copy in m1_arrival():
        copy.wait_recv()

    row8 = lax.broadcasted_iota(jnp.int32, (rows, chunk), 0)

    def local_terms(index, outside):
        cols = pl.ds(pl.multiple_of(index * chunk, 128), chunk)
        mid = pl.ds(pl.multiple_of(index * chunk + PAD, 128), chunk)
        wide = pl.ds(pl.multiple_of(index * chunk, 128), chunk + 2 * PAD)
        first_cond = 0.5 * recip(cond_x[layer_at(0) + 1, :, mid])
        wet = ponded[:, cols].astype(jnp.float32) * pond[:, cols]
        top = first_cond * (2.0 * (wet - head_x[layer_at(0) + 1, :, mid]) + 1.0)
        face_0 = jnp.where(is_top, 2.0 * first_cond, 0.0)
        flux_0 = jnp.where(is_top, top, jnp.where(depth == 3, -first_cond, 0.0))
        size = chunk + 2 * PAD
        most = chunk + PAD

        def step(place, carry):
            face_b, flux_b = carry
            layer = layer_at(place)
            slot = layer + 1
            cond_w = cond_x[slot, :, wide]
            head_w = head_x[slot, :, wide]
            cond = cond_w[:, PAD:PAD + chunk]
            here = head_w[:, PAD:PAD + chunk]
            face = series(cond, cond_x[slot + stride, :, mid])
            flux = face * (here - head_x[slot + stride, :, mid] + sign)
            cond_a = pltpu.roll(cond_w, size - 1, 1)[:, :most]
            head_a = pltpu.roll(head_w, size - 1, 1)[:, :most]
            along = series(cond_w[:, :most], cond_a) * (head_a - head_w[:, :most])
            lateral = along[:, PAD:] - pltpu.roll(along, 1, 1)[:, PAD:]
            across = series(cond, pltpu.roll(cond, rows - 1, 0)) * (pltpu.roll(here, rows - 1, 0) - here)
            across = jnp.where(row8 == rows - 1, 0.0, across)
            lateral = lateral + across - pltpu.roll(across, 1, 0)
            face_v[place, :, cols] = face
            sum_v[place, :, cols] = capd_v[layer, :, cols] + face + face_b
            rhs_v[place, :, cols] = flux_b - flux - base_v[layer, :, cols] + lateral
            return (face, flux)

        face, flux = lax.fori_loop(0, layers, step, (face_0, flux_0), unroll=4)
        last_v[:, cols] = flux
        return outside

    lax.fori_loop(0, count, local_terms, 0)

    def answer(index):
        cols = pl.ds(pl.multiple_of(index * chunk, 128), chunk)
        for _, side, _, answers in by_parity(index):
            @pl.when(answers)
            def _():
                ask_copy(1 - side, index).wait_recv()
                mine_h, mine_c = bsend[side, 0, :, cols], bsend[side, 1, :, cols]
                theirs_h, theirs_c = lrecv[0, :, cols], lrecv[1, :, cols]
                flux_v[side, :, cols] = series(mine_c, theirs_c) * (theirs_h - mine_h)
                answer_copy(side, index).start()

    def eliminate(index):
        cols = pl.ds(pl.multiple_of(index * chunk, 128), chunk)
        for side, _, asks, _ in by_parity(index):
            @pl.when(asks)
            def _():
                answer_arrival(side, index).wait_recv()
        turned = (1 - 2 * lax.rem(index, 2)).astype(jnp.float32)
        from_above = jnp.where(row8 == 0, turned, 0.0)
        from_below = jnp.where(row8 == rows - 1, -turned, 0.0)

        @pl.when(outer)
        def _():
            m2recv[0, :, cols] = jnp.zeros((rows, chunk), jnp.float32)
            m2recv[1, :, cols] = jnp.zeros((rows, chunk), jnp.float32)

        @pl.when(inner)
        def _():
            m2_copy(index).wait_recv()

        def step(place, carry):
            extra, inflow = carry
            layer = layer_at(place)
            above = flux_v[0, pl.ds(layer, 1), cols]
            below = flux_v[1, pl.ds(layer, 1), cols]
            lateral = from_above * above + from_below * below
            face = face_v[place, :, cols]
            scale = recip(sum_v[place, :, cols] + extra)
            ratio = face * scale
            value = (inflow + (rhs_v[place, :, cols] + lateral)) * scale
            y_v[place, :, cols] = value
            r_v[place, :, cols] = ratio
            return (-(face * ratio), face * value)

        extra, inflow = lax.fori_loop(
            0, layers, step, (m2recv[0, :, cols], m2recv[1, :, cols]), unroll=4
        )
        last = layers - 1
        nsend[0, :, cols] = jnp.where(outer, extra + face_v[last, :, cols], y_v[last, :, cols])
        nsend[1, :, cols] = jnp.where(outer, inflow + last_v[:, cols], r_v[last, :, cols])

        @pl.when(outer)
        def _():
            m2_copy(index).start()

        @pl.when(inner)
        def _():
            m3_copy(index).start()

    def substitute(index, beyond):
        cols = pl.ds(pl.multiple_of(index * chunk, 128), chunk)
        mid = pl.ds(pl.multiple_of(index * chunk + PAD, 128), chunk)

        def step(place, found):
            place = layers - 1 - place
            layer = layer_at(place)
            found = y_v[place, :, cols] + r_v[place, :, cols] * found
            out_v[layer, :, cols] = head_x[layer + 1, :, mid] + found
            return found

        found = lax.fori_loop(0, layers, step, beyond, unroll=4)
        return found

    def finish_inner(index):
        cols = pl.ds(pl.multiple_of(index * chunk, 128), chunk)
        m3_copy(index).wait_recv()
        y_own, r_own = nsend[0, :, cols], nsend[1, :, cols]
        y_far, r_far = m3recv[0, :, cols], m3recv[1, :, cols]
        m4send[:, cols] = substitute(index, (y_far + r_far * y_own) * recip(1.0 - r_own * r_far))
        m4_copy(index).start()

    def finish_outer(index):
        cols = pl.ds(pl.multiple_of(index * chunk, 128), chunk)
        m4_copy(index).wait_recv()
        substitute(index, m4recv[:, cols])

    def turn(index, carry):
        @pl.when(index < count)
        def _():
            answer(index)

        @pl.when((index >= 1) & (index <= count))
        def _():
            eliminate(index - 1)

        @pl.when(inner & (index >= 2) & (index <= count + 1))
        def _():
            finish_inner(index - 2)

        @pl.when(index == count + 2)
        def _():
            surface()

        @pl.when(outer & (index >= 3))
        def _():
            finish_outer(index - 3)

        return carry

    lax.fori_loop(0, count + 3, turn, 0)

    def drain(index, carry):
        for side, other, asks, answers in by_parity(index):
            @pl.when(asks)
            def _():
                ask_copy(side, index).wait_send()

            @pl.when(answers)
            def _():
                answer_copy(other, index).wait_send()

        @pl.when(outer)
        def _():
            m2_copy(index).wait_send()

        @pl.when(inner)
        def _():
            m3_copy(index).wait_send()
            m4_copy(index).wait_send()

        return carry

    lax.fori_loop(0, count, drain, 0)
    for side, present in ((0, has_up), (1, has_down)):
        @pl.when(present)
        def _():
            surf_copy(side).wait_send()

    @pl.when(inner)
    def _():
        for copy in m1_copy(1, middle) + m1_copy(0, partner):
            copy.wait_send()

    @pl.when(is_top)
    def _():
        for target in range(1, 4):
            x_copy(target).wait_send()


def per_device(lat_count, chunk, head, head_old, soil, cond_t, shape_t, pore_t, pond, ground, ponded, river):
    layers, rows, width = head.shape
    chunk = min(chunk, width)
    count = width // chunk
    strip = width // 4
    window = min(strip + 2 * PAD, width)
    f32 = jnp.float32
    padded = (layers + 2, rows, width + 2 * PAD)
    full = (layers, rows, width)
    plane = (rows, width)
    pair = (2, rows, width)
    any_spec = pl.BlockSpec(memory_space=pl.ANY)
    smem = pl.BlockSpec(memory_space=pltpu.SMEM)
    vmem = pl.BlockSpec(memory_space=pltpu.VMEM)
    dma = pltpu.SemaphoreType.DMA
    return pl.pallas_call(
        functools.partial(kernel, (layers, rows, width, lat_count, chunk)),
        out_shape=(pltpu.VMEM(full, f32), pltpu.VMEM((rows, strip), f32)),
        in_specs=[any_spec] * 3 + [smem] * 3 + [vmem] * 4,
        out_specs=(vmem, vmem),
        scratch_shapes=[
            pltpu.VMEM(padded, f32),
            pltpu.VMEM(padded, f32),
            pltpu.VMEM(full, f32),
            pltpu.VMEM(full, jnp.int32),
            pltpu.VMEM(full, f32),
            pltpu.VMEM(full, f32),
            pltpu.VMEM(full, f32),
            pltpu.VMEM(full, f32),
            pltpu.VMEM(full, f32),
            pltpu.VMEM(plane, f32),
            pltpu.VMEM(full, f32),
            pltpu.VMEM(full, f32),
            pltpu.VMEM((2, 2, layers, width), f32),
            pltpu.VMEM((2, layers, width), f32),
            pltpu.VMEM((2, layers, width), f32),
            pltpu.VMEM(pair, f32),
            pltpu.VMEM(pair, f32),
            pltpu.VMEM(pair, f32),
            pltpu.VMEM(plane, f32),
            pltpu.VMEM(plane, f32),
            pltpu.VMEM(plane, f32),
            pltpu.VMEM((rows, window), f32),
            pltpu.VMEM((2, 16, window), f32),
            pltpu.VMEM((2, 16, window), f32),
            pltpu.VMEM((4, rows + 8, window), f32),
            pltpu.VMEM((rows, window), f32),
            dma((3, count)),
            dma((count,)),
            dma((count,)),
            dma((count,)),
            dma((count,)),
            dma((2, 2)),
            dma((2,)),
            dma((count,)),
            dma((count,)),
            dma((count,)),
            dma((count,)),
            dma((count,)),
            dma((4,)),
            dma(()),
            dma((2,)),
            dma((2,)),
        ],
        compiler_params=pltpu.CompilerParams(
            collective_id=0, has_side_effects=True, vmem_limit_bytes=61 * 1024 * 1024
        ),
    )(head, head_old, soil, cond_t, shape_t, pore_t, pond, ground, ponded, river)


def solution(mesh):
    deep = P("depth", "lat", None)
    flat = P("lat", None)
    return jax.shard_map(
        functools.partial(per_device, mesh.shape["lat"], 512),
        mesh=mesh,
        in_specs=(deep, deep, deep, P(), P(), P(), flat, flat, flat, flat),
        out_specs=(deep, P("lat", "depth")),
        check_vma=False,
    )
```

```python
import functools

import jax
import jax.numpy as jnp
from jax import lax
from jax.experimental import pallas as pl
from jax.experimental.pallas import tpu as pltpu
from jax.sharding import PartitionSpec as P

SWEEPS = 4
TIME_STEP = 20.0
SURFACE_STEP = 2.0
SPECIFIC_STORAGE = 0.01
LAND_CONVEYANCE = 3.0
RIVER_CONVEYANCE = 10.0
SLOPE_FLOOR = 0.01
PAD = 128
TINY = 1e-30
CLOSED = 3e38
MESH = pl.DeviceIdType.MESH


def recip(value):
    guess = pl.reciprocal(value, approx=True)
    return guess * (2.0 - value * guess)


def harmonic(first, second):
    return 2.0 * first * second * recip(jnp.maximum(first + second, TINY))


def lane_table(table, scale):
    lane = lax.broadcasted_iota(jnp.int32, (8, 128), 1)
    value = jnp.zeros((8, 128), jnp.float32)
    for kind in range(table.shape[0]):
        value = jnp.where(lane == kind, scale * table[kind], value)
    return value


def lookup(soil, table):
    lines = []
    for top in range(0, soil.shape[0], 8):
        tiles = [
            jnp.take_along_axis(
                table, soil[top:top + 8, left:left + 128], axis=1, mode="promise_in_bounds"
            )
            for left in range(0, soil.shape[1], 128)
        ]
        lines.append(jnp.concatenate(tiles, axis=1))
    return lines[0] if len(lines) == 1 else jnp.concatenate(lines, axis=0)


def series(first, second):
    return recip(first + second)


def face_k(depth_face, slope, conveyance):
    power = jnp.exp((5.0 / 3.0) * jnp.log(jnp.maximum(depth_face, TINY)))
    return power * conveyance * lax.rsqrt(jnp.abs(slope) + SLOPE_FLOOR)


def kernel(
    sizes, head, head_old, soil, cond_t, shape_t, pore_t, pond, ground, ponded, river,
    out_v, surf,
    head_x, cond_x, old_v, soil_v, base_v, capd_v, face_v, rhs_v, sum_v, last_v, y_v, r_v,
    bsend, lrecv, flux_v, nsend, m2recv, m3recv, m4send, m4recv,
    top_v, xrecv, pack, srecv, sext, lev_v,
    in_sem, lat_s, lat_r, m1_s, m1_r, n_s, m2_r, m3_r, m4_s, m4_r,
    x_s, x_r, surf_s, surf_r,
):
    layers, rows, width, lat_count, chunk = sizes
    count = width // chunk
    strip = width // 4
    window = min(strip + 2 * PAD, width)
    lat = lax.axis_index("lat")
    depth = lax.axis_index("depth")
    has_up = lat > 0
    has_down = lat < lat_count - 1
    top_half = depth < 2
    is_top = depth == 0
    outer = (depth == 0) | (depth == 3)
    inner = (depth == 1) | (depth == 2)
    partner = jnp.where(top_half, 1 - depth, 5 - depth)
    middle = 3 - depth
    sign = jnp.where(top_half, 1.0, -1.0).astype(jnp.float32)
    stride = jnp.where(top_half, 1, -1)

    def layer_at(place):
        return jnp.where(top_half, place, layers - 1 - place)

    def start_of(index):
        return jnp.clip(index * strip - PAD, 0, width - window)

    body = pl.ds(PAD, width)
    def loads(part):
        cols = pl.ds(pl.multiple_of(part * chunk, 128), chunk)
        wide = pl.ds(pl.multiple_of(part * chunk + PAD, 128), chunk)
        return (
            pltpu.make_async_copy(head.at[:, :, cols], head_x.at[pl.ds(1, layers), :, wide], in_sem.at[0, part]),
            pltpu.make_async_copy(soil.at[:, :, cols], soil_v.at[:, :, cols], in_sem.at[1, part]),
            pltpu.make_async_copy(head_old.at[:, :, cols], old_v.at[:, :, cols], in_sem.at[2, part]),
        )

    def begin_loads(part, carry):
        for copy in loads(part):
            copy.start()
        return carry

    lax.fori_loop(0, count, begin_loads, 0)

    barrier = pltpu.get_barrier_semaphore()
    for shift in range(1, 4):
        pl.semaphore_signal(barrier, inc=1, device_id={"depth": lax.rem(depth + shift, 4)}, device_id_type=MESH)

    @pl.when(has_up)
    def _():
        pl.semaphore_signal(barrier, inc=1, device_id={"lat": lat - 1}, device_id_type=MESH)

    @pl.when(has_down)
    def _():
        pl.semaphore_signal(barrier, inc=1, device_id={"lat": lat + 1}, device_id_type=MESH)

    for field, value in ((head_x, 0.0), (cond_x, CLOSED)):
        filled = jnp.full((layers + 2, rows, PAD), value, jnp.float32)
        field[:, :, pl.ds(0, PAD)] = filled
        field[:, :, pl.ds(PAD + width, PAD)] = filled

    for side, present in ((0, has_up), (1, has_down)):
        @pl.when(jnp.logical_not(present))
        def _():
            lrecv[side, 0] = jnp.zeros(lrecv.shape[2:], jnp.float32)
            lrecv[side, 1] = jnp.full(lrecv.shape[2:], CLOSED, jnp.float32)
            srecv[side] = jnp.zeros(srecv.shape[1:], jnp.float32)

    pl.semaphore_wait(barrier, 3 + jnp.where(has_up, 1, 0) + jnp.where(has_down, 1, 0))

    def lat_copy(side, index):
        cols = pl.ds(pl.multiple_of(index * chunk, 128), chunk)
        return pltpu.make_async_remote_copy(
            src_ref=bsend.at[side, :, :, cols],
            dst_ref=lrecv.at[1 - side, :, :, cols],
            send_sem=lat_s.at[side, index],
            recv_sem=lat_r.at[1 - side, index],
            device_id={"lat": lat - 1 if side == 0 else lat + 1},
            device_id_type=MESH,
        )

    def lat_arrival(side, index):
        cols = pl.ds(pl.multiple_of(index * chunk, 128), chunk)
        return pltpu.make_async_remote_copy(
            src_ref=bsend.at[1 - side, :, :, cols],
            dst_ref=lrecv.at[side, :, :, cols],
            send_sem=lat_s.at[1 - side, index],
            recv_sem=lat_r.at[side, index],
            device_id={"lat": lat - 1 if side == 0 else lat + 1},
            device_id_type=MESH,
        )

    cond_l = lane_table(cond_t, 2.0)
    shape_l = lane_table(shape_t, 1.0)
    pore_l = lane_table(pore_t, 1.0)

    def states(part, carry):
        for copy in loads(part):
            copy.wait()
        cols = pl.ds(pl.multiple_of(part * chunk, 128), chunk)
        wide = pl.ds(pl.multiple_of(part * chunk + PAD, 128), chunk)

        def state(layer, passed):
            kinds = soil_v[layer, :, cols]
            steep, pore = lookup(kinds, shape_l), lookup(kinds, pore_l)
            now = head_x[layer + 1, :, wide]
            old = old_v[layer, :, cols]
            wet = jnp.exp(steep * jnp.minimum(now, 0.0))
            wet_old = jnp.exp(steep * jnp.minimum(old, 0.0))
            inverse = recip(lookup(kinds, cond_l) * wet)
            cond_x[layer + 1, :, wide] = inverse
            for side, row in ((0, 0), (1, rows - 1)):
                bsend[side, 0, pl.ds(layer, 1), cols] = now[row:row + 1]
                bsend[side, 1, pl.ds(layer, 1), cols] = inverse[row:row + 1]
            change = pore * (wet - wet_old) + SPECIFIC_STORAGE * (now - old)
            base_v[layer, :, cols] = change * (1.0 / TIME_STEP)
            capd_v[layer, :, cols] = (SPECIFIC_STORAGE + pore * steep * wet) * (1.0 / TIME_STEP)
            return passed

        lax.fori_loop(0, layers, state, 0, unroll=4)
        for side, present in ((0, has_up), (1, has_down)):
            @pl.when(present)
            def _():
                lat_copy(side, part).start()
        return carry

    lax.fori_loop(0, count, states, 0)

    def m1_copy(place, target):
        slot = jnp.where(top_half, layers + 1, 0) if place == 0 else jnp.where(top_half, 0, layers + 1)
        layer = layer_at(0 if place == 0 else layers - 1) + 1
        return [
            pltpu.make_async_remote_copy(
                src_ref=field.at[layer, :, body],
                dst_ref=field.at[slot, :, body],
                send_sem=m1_s.at[place, which],
                recv_sem=m1_r.at[which],
                device_id={"depth": target},
                device_id_type=MESH,
            )
            for which, field in enumerate((head_x, cond_x))
        ]

    def m1_arrival():
        slot = jnp.where(top_half, layers + 1, 0)
        layer = layer_at(layers - 1) + 1
        return [
            pltpu.make_async_remote_copy(
                src_ref=field.at[layer, :, body],
                dst_ref=field.at[slot, :, body],
                send_sem=m1_s.at[1, which],
                recv_sem=m1_r.at[which],
                device_id={"depth": partner},
                device_id_type=MESH,
            )
            for which, field in enumerate((head_x, cond_x))
        ]

    @pl.when(inner)
    def _():
        for copy in m1_copy(1, middle):
            copy.start()
        for copy in m1_copy(0, partner):
            copy.start()

    def x_copy(target):
        return pltpu.make_async_remote_copy(
            src_ref=top_v.at[:, pl.ds(min(max(target * strip - PAD, 0), width - window), window)],
            dst_ref=xrecv,
            send_sem=x_s.at[target],
            recv_sem=x_r,
            device_id={"depth": target},
            device_id_type=MESH,
        )

    @pl.when(is_top)
    def _():
        wet = ponded[...].astype(jnp.float32) * pond[...]
        top_v[...] = 0.5 * recip(cond_x[1, :, body]) * (2.0 * (wet - head_x[1, :, body]) + 1.0)
        for target in range(1, 4):
            x_copy(target).start()
        xrecv[...] = top_v[:, pl.ds(0, window)]

    @pl.when(jnp.logical_not(is_top))
    def _():
        x_copy(1).wait_recv()

    begin = pl.multiple_of(start_of(depth), 128)
    view = pl.ds(begin, window)
    conveyance = LAND_CONVEYANCE + (RIVER_CONVEYANCE - LAND_CONVEYANCE) * river[:, view].astype(jnp.float32)
    own = (pond[:, view], ground[:, view], conveyance, -xrecv[...])
    for place, value in enumerate(own):
        for side, first in ((0, 0), (1, rows - 4)):
            pack[side, pl.ds(4 * place, 4), :] = value[first:first + 4]
        sext[place, pl.ds(4, rows), :] = value

    def surf_copy(side):
        return pltpu.make_async_remote_copy(
            src_ref=pack.at[side],
            dst_ref=srecv.at[1 - side],
            send_sem=surf_s.at[side],
            recv_sem=surf_r.at[1 - side],
            device_id={"lat": lat - 1 if side == 0 else lat + 1},
            device_id_type=MESH,
        )

    def surf_arrival(side):
        return pltpu.make_async_remote_copy(
            src_ref=pack.at[1 - side],
            dst_ref=srecv.at[side],
            send_sem=surf_s.at[1 - side],
            recv_sem=surf_r.at[side],
            device_id={"lat": lat - 1 if side == 0 else lat + 1},
            device_id_type=MESH,
        )

    for side, present in ((0, has_up), (1, has_down)):
        @pl.when(present)
        def _():
            surf_copy(side).start()

    def surface():
        for side, present in ((0, has_up), (1, has_down)):
            @pl.when(present)
            def _():
                surf_arrival(side).wait_recv()
        for place in range(4):
            sext[place, pl.ds(0, 4), :] = srecv[0, pl.ds(4 * place, 4), :]
            sext[place, pl.ds(4 + rows, 4), :] = srecv[1, pl.ds(4 * place, 4), :]
        tall = rows + 8
        depth_w, ground_w, conv_w, exfil = (sext[place] for place in range(4))
        row = lax.broadcasted_iota(jnp.int32, (tall, window), 0)
        col = lax.broadcasted_iota(jnp.int32, (tall, window), 1)

        def after(value, axis):
            return pltpu.roll(value, value.shape[axis] - 1, axis)

        def before(value, axis):
            return pltpu.roll(value, 1, axis)

        total = jnp.full((tall, window), 1.0 / SURFACE_STEP, jnp.float32)
        rhs = depth_w * (1.0 / SURFACE_STEP) + exfil
        faces = []
        for axis, last in ((0, row == tall - 1), (1, col == window - 1)):
            depth_n, ground_n, conv_n = (after(value, axis) for value in (depth_w, ground_w, conv_w))
            k = face_k(
                0.5 * (depth_w + depth_n),
                depth_n + ground_n - (depth_w + ground_w),
                harmonic(conv_w, conv_n),
            )
            k = jnp.where(last, 0.0, k)
            k_before = before(k, axis)
            flow = k * (ground_n - ground_w)
            total = total + k + k_before
            rhs = rhs + flow - before(flow, axis)
            faces.append((axis, k, k_before))
        scale = recip(total)
        level = depth_w
        for _ in range(SWEEPS):
            fed = rhs
            for axis, k, k_before in faces:
                fed = fed + k * after(level, axis) + k_before * before(level, axis)
            level = fed * scale
        lev_v[...] = level[4:4 + rows]
        offset = pl.multiple_of(depth * strip - begin, 128)
        surf[...] = lev_v[:, pl.ds(offset, strip)]

    def m2_copy(index):
        cols = pl.ds(pl.multiple_of(index * chunk, 128), chunk)
        return pltpu.make_async_remote_copy(
            src_ref=nsend.at[:, :, cols], dst_ref=m2recv.at[:, :, cols],
            send_sem=n_s.at[index], recv_sem=m2_r.at[index],
            device_id={"depth": partner}, device_id_type=MESH,
        )

    def m3_copy(index):
        cols = pl.ds(pl.multiple_of(index * chunk, 128), chunk)
        return pltpu.make_async_remote_copy(
            src_ref=nsend.at[:, :, cols], dst_ref=m3recv.at[:, :, cols],
            send_sem=n_s.at[index], recv_sem=m3_r.at[index],
            device_id={"depth": middle}, device_id_type=MESH,
        )

    def m4_copy(index):
        cols = pl.ds(pl.multiple_of(index * chunk, 128), chunk)
        return pltpu.make_async_remote_copy(
            src_ref=m4send.at[:, cols], dst_ref=m4recv.at[:, cols],
            send_sem=m4_s.at[index], recv_sem=m4_r.at[index],
            device_id={"depth": partner}, device_id_type=MESH,
        )

    for copy in m1_arrival():
        copy.wait_recv()

    row8 = lax.broadcasted_iota(jnp.int32, (rows, chunk), 0)

    def local_terms(index, outside):
        cols = pl.ds(pl.multiple_of(index * chunk, 128), chunk)
        mid = pl.ds(pl.multiple_of(index * chunk + PAD, 128), chunk)
        wide = pl.ds(pl.multiple_of(index * chunk, 128), chunk + 2 * PAD)
        first_cond = 0.5 * recip(cond_x[layer_at(0) + 1, :, mid])
        wet = ponded[:, cols].astype(jnp.float32) * pond[:, cols]
        top = first_cond * (2.0 * (wet - head_x[layer_at(0) + 1, :, mid]) + 1.0)
        face_0 = jnp.where(is_top, 2.0 * first_cond, 0.0)
        flux_0 = jnp.where(is_top, top, jnp.where(depth == 3, -first_cond, 0.0))
        size = chunk + 2 * PAD
        most = chunk + PAD

        def step(place, carry):
            face_b, flux_b = carry
            layer = layer_at(place)
            slot = layer + 1
            cond_w = cond_x[slot, :, wide]
            head_w = head_x[slot, :, wide]
            cond = cond_w[:, PAD:PAD + chunk]
            here = head_w[:, PAD:PAD + chunk]
            face = series(cond, cond_x[slot + stride, :, mid])
            flux = face * (here - head_x[slot + stride, :, mid] + sign)
            cond_a = pltpu.roll(cond_w, size - 1, 1)[:, :most]
            head_a = pltpu.roll(head_w, size - 1, 1)[:, :most]
            along = series(cond_w[:, :most], cond_a) * (head_a - head_w[:, :most])
            lateral = along[:, PAD:] - pltpu.roll(along, 1, 1)[:, PAD:]
            across = series(cond, pltpu.roll(cond, rows - 1, 0)) * (pltpu.roll(here, rows - 1, 0) - here)
            across = jnp.where(row8 == rows - 1, 0.0, across)
            lateral = lateral + across - pltpu.roll(across, 1, 0)
            face_v[place, :, cols] = face
            sum_v[place, :, cols] = capd_v[layer, :, cols] + face + face_b
            rhs_v[place, :, cols] = flux_b - flux - base_v[layer, :, cols] + lateral
            return (face, flux)

        face, flux = lax.fori_loop(0, layers, step, (face_0, flux_0), unroll=4)
        last_v[:, cols] = flux
        return outside

    lax.fori_loop(0, count, local_terms, 0)

    def eliminate(index):
        cols = pl.ds(pl.multiple_of(index * chunk, 128), chunk)
        for side, present in ((0, has_up), (1, has_down)):
            @pl.when(present)
            def _():
                lat_arrival(side, index).wait_recv()
            mine_h, mine_c = bsend[side, 0, :, cols], bsend[side, 1, :, cols]
            theirs_h, theirs_c = lrecv[side, 0, :, cols], lrecv[side, 1, :, cols]
            flux_v[side] = series(mine_c, theirs_c) * (theirs_h - mine_h)

        @pl.when(outer)
        def _():
            m2recv[0, :, cols] = jnp.zeros((rows, chunk), jnp.float32)
            m2recv[1, :, cols] = jnp.zeros((rows, chunk), jnp.float32)

        @pl.when(inner)
        def _():
            m2_copy(index).wait_recv()

        def step(place, carry):
            extra, inflow = carry
            layer = layer_at(place)
            above = flux_v[0, pl.ds(layer, 1), :]
            below = flux_v[1, pl.ds(layer, 1), :]
            lateral = jnp.where(row8 == 0, above, jnp.where(row8 == rows - 1, below, 0.0))
            face = face_v[place, :, cols]
            scale = recip(sum_v[place, :, cols] + extra)
            ratio = face * scale
            value = (inflow + (rhs_v[place, :, cols] + lateral)) * scale
            y_v[place, :, cols] = value
            r_v[place, :, cols] = ratio
            return (-(face * ratio), face * value)

        extra, inflow = lax.fori_loop(
            0, layers, step, (m2recv[0, :, cols], m2recv[1, :, cols]), unroll=4
        )
        last = layers - 1
        nsend[0, :, cols] = jnp.where(outer, extra + face_v[last, :, cols], y_v[last, :, cols])
        nsend[1, :, cols] = jnp.where(outer, inflow + last_v[:, cols], r_v[last, :, cols])

        @pl.when(outer)
        def _():
            m2_copy(index).start()

        @pl.when(inner)
        def _():
            m3_copy(index).start()

    def substitute(index, beyond):
        cols = pl.ds(pl.multiple_of(index * chunk, 128), chunk)
        mid = pl.ds(pl.multiple_of(index * chunk + PAD, 128), chunk)

        def step(place, found):
            place = layers - 1 - place
            layer = layer_at(place)
            found = y_v[place, :, cols] + r_v[place, :, cols] * found
            out_v[layer, :, cols] = head_x[layer + 1, :, mid] + found
            return found

        found = lax.fori_loop(0, layers, step, beyond, unroll=4)
        return found

    def finish_inner(index):
        cols = pl.ds(pl.multiple_of(index * chunk, 128), chunk)
        m3_copy(index).wait_recv()
        y_own, r_own = nsend[0, :, cols], nsend[1, :, cols]
        y_far, r_far = m3recv[0, :, cols], m3recv[1, :, cols]
        m4send[:, cols] = substitute(index, (y_far + r_far * y_own) * recip(1.0 - r_own * r_far))
        m4_copy(index).start()

    def finish_outer(index):
        cols = pl.ds(pl.multiple_of(index * chunk, 128), chunk)
        m4_copy(index).wait_recv()
        substitute(index, m4recv[:, cols])

    lag = 5

    def turn(index, carry):
        @pl.when(index < count)
        def _():
            eliminate(index)

        @pl.when(inner & (index >= 2) & (index < count + 2))
        def _():
            finish_inner(index - 2)

        @pl.when(index == jnp.where(outer, count, count + 2))
        def _():
            surface()

        @pl.when(outer & (index >= lag))
        def _():
            finish_outer(index - lag)

        return carry

    lax.fori_loop(0, count + lag, turn, 0)

    def drain(index, carry):
        for side, present in ((0, has_up), (1, has_down)):
            @pl.when(present)
            def _():
                lat_copy(side, index).wait_send()

        @pl.when(outer)
        def _():
            m2_copy(index).wait_send()

        @pl.when(inner)
        def _():
            m3_copy(index).wait_send()
            m4_copy(index).wait_send()

        return carry

    lax.fori_loop(0, count, drain, 0)
    for side, present in ((0, has_up), (1, has_down)):
        @pl.when(present)
        def _():
            surf_copy(side).wait_send()

    @pl.when(inner)
    def _():
        for copy in m1_copy(1, middle) + m1_copy(0, partner):
            copy.wait_send()

    @pl.when(is_top)
    def _():
        for target in range(1, 4):
            x_copy(target).wait_send()


def per_device(lat_count, chunk, head, head_old, soil, cond_t, shape_t, pore_t, pond, ground, ponded, river):
    layers, rows, width = head.shape
    chunk = min(chunk, width)
    count = width // chunk
    strip = width // 4
    window = min(strip + 2 * PAD, width)
    f32 = jnp.float32
    padded = (layers + 2, rows, width + 2 * PAD)
    full = (layers, rows, width)
    plane = (rows, width)
    pair = (2, rows, width)
    any_spec = pl.BlockSpec(memory_space=pl.ANY)
    smem = pl.BlockSpec(memory_space=pltpu.SMEM)
    vmem = pl.BlockSpec(memory_space=pltpu.VMEM)
    dma = pltpu.SemaphoreType.DMA
    return pl.pallas_call(
        functools.partial(kernel, (layers, rows, width, lat_count, chunk)),
        out_shape=(pltpu.VMEM(full, f32), pltpu.VMEM((rows, strip), f32)),
        in_specs=[any_spec] * 3 + [smem] * 3 + [vmem] * 4,
        out_specs=(vmem, vmem),
        scratch_shapes=[
            pltpu.VMEM(padded, f32),
            pltpu.VMEM(padded, f32),
            pltpu.VMEM(full, f32),
            pltpu.VMEM(full, jnp.int32),
            pltpu.VMEM(full, f32),
            pltpu.VMEM(full, f32),
            pltpu.VMEM(full, f32),
            pltpu.VMEM(full, f32),
            pltpu.VMEM(full, f32),
            pltpu.VMEM(plane, f32),
            pltpu.VMEM(full, f32),
            pltpu.VMEM(full, f32),
            pltpu.VMEM((2, 2, layers, width), f32),
            pltpu.VMEM((2, 2, layers, width), f32),
            pltpu.VMEM((2, layers, chunk), f32),
            pltpu.VMEM(pair, f32),
            pltpu.VMEM(pair, f32),
            pltpu.VMEM(pair, f32),
            pltpu.VMEM(plane, f32),
            pltpu.VMEM(plane, f32),
            pltpu.VMEM(plane, f32),
            pltpu.VMEM((rows, window), f32),
            pltpu.VMEM((2, 16, window), f32),
            pltpu.VMEM((2, 16, window), f32),
            pltpu.VMEM((4, rows + 8, window), f32),
            pltpu.VMEM((rows, window), f32),
            dma((3, count)),
            dma((2, count)),
            dma((2, count)),
            dma((2, 2)),
            dma((2,)),
            dma((count,)),
            dma((count,)),
            dma((count,)),
            dma((count,)),
            dma((count,)),
            dma((4,)),
            dma(()),
            dma((2,)),
            dma((2,)),
        ],
        compiler_params=pltpu.CompilerParams(
            collective_id=0, has_side_effects=True, vmem_limit_bytes=61 * 1024 * 1024
        ),
    )(head, head_old, soil, cond_t, shape_t, pore_t, pond, ground, ponded, river)


def solution(mesh):
    deep = P("depth", "lat", None)
    flat = P("lat", None)
    return jax.shard_map(
        functools.partial(per_device, mesh.shape["lat"], 512),
        mesh=mesh,
        in_specs=(deep, deep, deep, P(), P(), P(), flat, flat, flat, flat),
        out_specs=(deep, P("lat", "depth")),
        check_vma=False,
    )
```

```python
import functools

import jax
import jax.numpy as jnp
from jax import lax
from jax.experimental import pallas as pl
from jax.experimental.pallas import tpu as pltpu
from jax.sharding import PartitionSpec as P

SWEEPS = 4
TIME_STEP = 20.0
SURFACE_STEP = 2.0
SPECIFIC_STORAGE = 0.01
LAND_CONVEYANCE = 3.0
RIVER_CONVEYANCE = 10.0
SLOPE_FLOOR = 0.01
PAD = 128
TINY = 1e-30
CLOSED = 3e38
MESH = pl.DeviceIdType.MESH


def recip(value):
    guess = pl.reciprocal(value, approx=True)
    return guess * (2.0 - value * guess)


def harmonic(first, second):
    return 2.0 * first * second * recip(jnp.maximum(first + second, TINY))


def lane_table(table, scale):
    lane = lax.broadcasted_iota(jnp.int32, (8, 128), 1)
    value = jnp.zeros((8, 128), jnp.float32)
    for kind in range(table.shape[0]):
        value = jnp.where(lane == kind, scale * table[kind], value)
    return value


def lookup(soil, table):
    lines = []
    for top in range(0, soil.shape[0], 8):
        tiles = [
            jnp.take_along_axis(
                table, soil[top:top + 8, left:left + 128], axis=1, mode="promise_in_bounds"
            )
            for left in range(0, soil.shape[1], 128)
        ]
        lines.append(jnp.concatenate(tiles, axis=1))
    return lines[0] if len(lines) == 1 else jnp.concatenate(lines, axis=0)


def series(first, second):
    return recip(first + second)


def face_k(depth_face, slope, conveyance):
    power = jnp.exp((5.0 / 3.0) * jnp.log(jnp.maximum(depth_face, TINY)))
    return power * conveyance * lax.rsqrt(jnp.abs(slope) + SLOPE_FLOOR)


def kernel(
    sizes, head, head_old, soil, cond_t, shape_t, pore_t, pond, ground, ponded, river,
    out_v, surf,
    head_x, cond_x, old_v, soil_v, base_v, capd_v, face_v, rhs_v, sum_v, last_v, y_v, r_v,
    bsend, lrecv, flux_v, nsend, m2recv, m3recv, m4send, m4recv,
    top_v, xrecv, pack, srecv, sext, lev_v,
    in_sem, lat_s, lat_r, m1_s, m1_r, n_s, m2_r, m3_r, m4_s, m4_r,
    x_s, x_r, surf_s, surf_r,
):
    layers, rows, width, lat_count, chunk = sizes
    count = width // chunk
    strip = width // 4
    window = min(strip + 2 * PAD, width)
    lat = lax.axis_index("lat")
    depth = lax.axis_index("depth")
    has_up = lat > 0
    has_down = lat < lat_count - 1
    top_half = depth < 2
    is_top = depth == 0
    outer = (depth == 0) | (depth == 3)
    inner = (depth == 1) | (depth == 2)
    partner = jnp.where(top_half, 1 - depth, 5 - depth)
    middle = 3 - depth
    sign = jnp.where(top_half, 1.0, -1.0).astype(jnp.float32)
    stride = jnp.where(top_half, 1, -1)

    def layer_at(place):
        return jnp.where(top_half, place, layers - 1 - place)

    def start_of(index):
        return jnp.clip(index * strip - PAD, 0, width - window)

    body = pl.ds(PAD, width)
    def loads(part):
        cols = pl.ds(pl.multiple_of(part * chunk, 128), chunk)
        wide = pl.ds(pl.multiple_of(part * chunk + PAD, 128), chunk)
        return (
            pltpu.make_async_copy(head.at[:, :, cols], head_x.at[pl.ds(1, layers), :, wide], in_sem.at[0, part]),
            pltpu.make_async_copy(soil.at[:, :, cols], soil_v.at[:, :, cols], in_sem.at[1, part]),
            pltpu.make_async_copy(head_old.at[:, :, cols], old_v.at[:, :, cols], in_sem.at[2, part]),
        )

    def begin_loads(part, carry):
        for copy in loads(part):
            copy.start()
        return carry

    lax.fori_loop(0, count, begin_loads, 0)

    barrier = pltpu.get_barrier_semaphore()
    for shift in range(1, 4):
        pl.semaphore_signal(barrier, inc=1, device_id={"depth": lax.rem(depth + shift, 4)}, device_id_type=MESH)

    @pl.when(has_up)
    def _():
        pl.semaphore_signal(barrier, inc=1, device_id={"lat": lat - 1}, device_id_type=MESH)

    @pl.when(has_down)
    def _():
        pl.semaphore_signal(barrier, inc=1, device_id={"lat": lat + 1}, device_id_type=MESH)

    for field, value in ((head_x, 0.0), (cond_x, CLOSED)):
        filled = jnp.full((layers + 2, rows, PAD), value, jnp.float32)
        field[:, :, pl.ds(0, PAD)] = filled
        field[:, :, pl.ds(PAD + width, PAD)] = filled

    for side, present in ((0, has_up), (1, has_down)):
        @pl.when(jnp.logical_not(present))
        def _():
            lrecv[side, 0] = jnp.zeros(lrecv.shape[2:], jnp.float32)
            lrecv[side, 1] = jnp.full(lrecv.shape[2:], CLOSED, jnp.float32)
            srecv[side] = jnp.zeros(srecv.shape[1:], jnp.float32)

    pl.semaphore_wait(barrier, 3 + jnp.where(has_up, 1, 0) + jnp.where(has_down, 1, 0))

    def lat_copy(side, index):
        cols = pl.ds(pl.multiple_of(index * chunk, 128), chunk)
        return pltpu.make_async_remote_copy(
            src_ref=bsend.at[side, :, :, cols],
            dst_ref=lrecv.at[1 - side, :, :, cols],
            send_sem=lat_s.at[side, index],
            recv_sem=lat_r.at[1 - side, index],
            device_id={"lat": lat - 1 if side == 0 else lat + 1},
            device_id_type=MESH,
        )

    def lat_arrival(side, index):
        cols = pl.ds(pl.multiple_of(index * chunk, 128), chunk)
        return pltpu.make_async_remote_copy(
            src_ref=bsend.at[1 - side, :, :, cols],
            dst_ref=lrecv.at[side, :, :, cols],
            send_sem=lat_s.at[1 - side, index],
            recv_sem=lat_r.at[side, index],
            device_id={"lat": lat - 1 if side == 0 else lat + 1},
            device_id_type=MESH,
        )

    cond_l = lane_table(cond_t, 2.0)
    shape_l = lane_table(shape_t, 1.0)
    pore_l = lane_table(pore_t, 1.0)

    def m1_copies(place, target, part):
        slot = jnp.where(top_half, layers + 1, 0) if place == 0 else jnp.where(top_half, 0, layers + 1)
        layer = layer_at(0 if place == 0 else layers - 1) + 1
        wide = pl.ds(pl.multiple_of(part * chunk + PAD, 128), chunk)
        return [
            pltpu.make_async_remote_copy(
                src_ref=field.at[layer, :, wide],
                dst_ref=field.at[slot, :, wide],
                send_sem=m1_s.at[place, which, part],
                recv_sem=m1_r.at[which, part],
                device_id={"depth": target},
                device_id_type=MESH,
            )
            for which, field in enumerate((head_x, cond_x))
        ]

    def m1_sends(part):
        return m1_copies(1, middle, part) + m1_copies(0, partner, part)

    def m1_arrivals(part):
        slot = jnp.where(top_half, layers + 1, 0)
        layer = layer_at(layers - 1) + 1
        wide = pl.ds(pl.multiple_of(part * chunk + PAD, 128), chunk)
        return [
            pltpu.make_async_remote_copy(
                src_ref=field.at[layer, :, wide],
                dst_ref=field.at[slot, :, wide],
                send_sem=m1_s.at[1, which, part],
                recv_sem=m1_r.at[which, part],
                device_id={"depth": partner},
                device_id_type=MESH,
            )
            for which, field in enumerate((head_x, cond_x))
        ]

    def states(part, carry):
        for copy in loads(part):
            copy.wait()
        cols = pl.ds(pl.multiple_of(part * chunk, 128), chunk)
        wide = pl.ds(pl.multiple_of(part * chunk + PAD, 128), chunk)

        def state(layer, passed):
            kinds = soil_v[layer, :, cols]
            steep, pore = lookup(kinds, shape_l), lookup(kinds, pore_l)
            now = head_x[layer + 1, :, wide]
            old = old_v[layer, :, cols]
            wet = jnp.exp(steep * jnp.minimum(now, 0.0))
            wet_old = jnp.exp(steep * jnp.minimum(old, 0.0))
            inverse = recip(lookup(kinds, cond_l) * wet)
            cond_x[layer + 1, :, wide] = inverse
            for side, row in ((0, 0), (1, rows - 1)):
                bsend[side, 0, pl.ds(layer, 1), cols] = now[row:row + 1]
                bsend[side, 1, pl.ds(layer, 1), cols] = inverse[row:row + 1]
            change = pore * (wet - wet_old) + SPECIFIC_STORAGE * (now - old)
            base_v[layer, :, cols] = change * (1.0 / TIME_STEP)
            capd_v[layer, :, cols] = (SPECIFIC_STORAGE + pore * steep * wet) * (1.0 / TIME_STEP)
            return passed

        lax.fori_loop(0, layers, state, 0, unroll=4)
        for side, present in ((0, has_up), (1, has_down)):
            @pl.when(present)
            def _():
                lat_copy(side, part).start()

        @pl.when(inner)
        def _():
            for copy in m1_sends(part):
                copy.start()
        return carry

    lax.fori_loop(0, count, states, 0)

    def x_copy(target):
        return pltpu.make_async_remote_copy(
            src_ref=top_v.at[:, pl.ds(min(max(target * strip - PAD, 0), width - window), window)],
            dst_ref=xrecv,
            send_sem=x_s.at[target],
            recv_sem=x_r,
            device_id={"depth": target},
            device_id_type=MESH,
        )

    @pl.when(is_top)
    def _():
        wet = ponded[...].astype(jnp.float32) * pond[...]
        top_v[...] = 0.5 * recip(cond_x[1, :, body]) * (2.0 * (wet - head_x[1, :, body]) + 1.0)
        for target in range(1, 4):
            x_copy(target).start()
        xrecv[...] = top_v[:, pl.ds(0, window)]

    def m2_copy(index):
        cols = pl.ds(pl.multiple_of(index * chunk, 128), chunk)
        return pltpu.make_async_remote_copy(
            src_ref=nsend.at[:, :, cols], dst_ref=m2recv.at[:, :, cols],
            send_sem=n_s.at[index], recv_sem=m2_r.at[index],
            device_id={"depth": partner}, device_id_type=MESH,
        )

    def m3_copy(index):
        cols = pl.ds(pl.multiple_of(index * chunk, 128), chunk)
        return pltpu.make_async_remote_copy(
            src_ref=nsend.at[:, :, cols], dst_ref=m3recv.at[:, :, cols],
            send_sem=n_s.at[index], recv_sem=m3_r.at[index],
            device_id={"depth": middle}, device_id_type=MESH,
        )

    def m4_copy(index):
        cols = pl.ds(pl.multiple_of(index * chunk, 128), chunk)
        return pltpu.make_async_remote_copy(
            src_ref=m4send.at[:, cols], dst_ref=m4recv.at[:, cols],
            send_sem=m4_s.at[index], recv_sem=m4_r.at[index],
            device_id={"depth": partner}, device_id_type=MESH,
        )

    row8 = lax.broadcasted_iota(jnp.int32, (rows, chunk), 0)

    def local_terms(index, outside):
        for copy in m1_arrivals(index):
            copy.wait_recv()
        cols = pl.ds(pl.multiple_of(index * chunk, 128), chunk)
        mid = pl.ds(pl.multiple_of(index * chunk + PAD, 128), chunk)
        wide = pl.ds(pl.multiple_of(index * chunk, 128), chunk + 2 * PAD)
        first_cond = 0.5 * recip(cond_x[layer_at(0) + 1, :, mid])
        wet = ponded[:, cols].astype(jnp.float32) * pond[:, cols]
        top = first_cond * (2.0 * (wet - head_x[layer_at(0) + 1, :, mid]) + 1.0)
        face_0 = jnp.where(is_top, 2.0 * first_cond, 0.0)
        flux_0 = jnp.where(is_top, top, jnp.where(depth == 3, -first_cond, 0.0))
        size = chunk + 2 * PAD
        most = chunk + PAD

        def step(place, carry):
            face_b, flux_b = carry
            layer = layer_at(place)
            slot = layer + 1
            cond_w = cond_x[slot, :, wide]
            head_w = head_x[slot, :, wide]
            cond = cond_w[:, PAD:PAD + chunk]
            here = head_w[:, PAD:PAD + chunk]
            face = series(cond, cond_x[slot + stride, :, mid])
            flux = face * (here - head_x[slot + stride, :, mid] + sign)
            cond_a = pltpu.roll(cond_w, size - 1, 1)[:, :most]
            head_a = pltpu.roll(head_w, size - 1, 1)[:, :most]
            along = series(cond_w[:, :most], cond_a) * (head_a - head_w[:, :most])
            lateral = along[:, PAD:] - pltpu.roll(along, 1, 1)[:, PAD:]
            across = series(cond, pltpu.roll(cond, rows - 1, 0)) * (pltpu.roll(here, rows - 1, 0) - here)
            across = jnp.where(row8 == rows - 1, 0.0, across)
            lateral = lateral + across - pltpu.roll(across, 1, 0)
            face_v[place, :, cols] = face
            sum_v[place, :, cols] = capd_v[layer, :, cols] + face + face_b
            rhs_v[place, :, cols] = flux_b - flux - base_v[layer, :, cols] + lateral
            return (face, flux)

        face, flux = lax.fori_loop(0, layers, step, (face_0, flux_0), unroll=4)
        last_v[:, cols] = flux
        return outside

    lax.fori_loop(0, count, local_terms, 0)

    @pl.when(jnp.logical_not(is_top))
    def _():
        x_copy(1).wait_recv()

    begin = pl.multiple_of(start_of(depth), 128)
    view = pl.ds(begin, window)
    conveyance = LAND_CONVEYANCE + (RIVER_CONVEYANCE - LAND_CONVEYANCE) * river[:, view].astype(jnp.float32)
    own = (pond[:, view], ground[:, view], conveyance, -xrecv[...])
    for place, value in enumerate(own):
        for side, first in ((0, 0), (1, rows - 4)):
            pack[side, pl.ds(4 * place, 4), :] = value[first:first + 4]
        sext[place, pl.ds(4, rows), :] = value

    def surf_copy(side):
        return pltpu.make_async_remote_copy(
            src_ref=pack.at[side],
            dst_ref=srecv.at[1 - side],
            send_sem=surf_s.at[side],
            recv_sem=surf_r.at[1 - side],
            device_id={"lat": lat - 1 if side == 0 else lat + 1},
            device_id_type=MESH,
        )

    def surf_arrival(side):
        return pltpu.make_async_remote_copy(
            src_ref=pack.at[1 - side],
            dst_ref=srecv.at[side],
            send_sem=surf_s.at[1 - side],
            recv_sem=surf_r.at[side],
            device_id={"lat": lat - 1 if side == 0 else lat + 1},
            device_id_type=MESH,
        )

    for side, present in ((0, has_up), (1, has_down)):
        @pl.when(present)
        def _():
            surf_copy(side).start()

    def surface():
        for side, present in ((0, has_up), (1, has_down)):
            @pl.when(present)
            def _():
                surf_arrival(side).wait_recv()
        for place in range(4):
            sext[place, pl.ds(0, 4), :] = srecv[0, pl.ds(4 * place, 4), :]
            sext[place, pl.ds(4 + rows, 4), :] = srecv[1, pl.ds(4 * place, 4), :]
        tall = rows + 8
        depth_w, ground_w, conv_w, exfil = (sext[place] for place in range(4))
        row = lax.broadcasted_iota(jnp.int32, (tall, window), 0)
        col = lax.broadcasted_iota(jnp.int32, (tall, window), 1)

        def after(value, axis):
            return pltpu.roll(value, value.shape[axis] - 1, axis)

        def before(value, axis):
            return pltpu.roll(value, 1, axis)

        total = jnp.full((tall, window), 1.0 / SURFACE_STEP, jnp.float32)
        rhs = depth_w * (1.0 / SURFACE_STEP) + exfil
        faces = []
        for axis, last in ((0, row == tall - 1), (1, col == window - 1)):
            depth_n, ground_n, conv_n = (after(value, axis) for value in (depth_w, ground_w, conv_w))
            k = face_k(
                0.5 * (depth_w + depth_n),
                depth_n + ground_n - (depth_w + ground_w),
                harmonic(conv_w, conv_n),
            )
            k = jnp.where(last, 0.0, k)
            k_before = before(k, axis)
            flow = k * (ground_n - ground_w)
            total = total + k + k_before
            rhs = rhs + flow - before(flow, axis)
            faces.append((axis, k, k_before))
        scale = recip(total)
        level = depth_w
        for _ in range(SWEEPS):
            fed = rhs
            for axis, k, k_before in faces:
                fed = fed + k * after(level, axis) + k_before * before(level, axis)
            level = fed * scale
        lev_v[...] = level[4:4 + rows]
        offset = pl.multiple_of(depth * strip - begin, 128)
        surf[...] = lev_v[:, pl.ds(offset, strip)]

    def eliminate(index):
        cols = pl.ds(pl.multiple_of(index * chunk, 128), chunk)
        for side, present in ((0, has_up), (1, has_down)):
            @pl.when(present)
            def _():
                lat_arrival(side, index).wait_recv()
            mine_h, mine_c = bsend[side, 0, :, cols], bsend[side, 1, :, cols]
            theirs_h, theirs_c = lrecv[side, 0, :, cols], lrecv[side, 1, :, cols]
            flux_v[side] = series(mine_c, theirs_c) * (theirs_h - mine_h)

        @pl.when(outer)
        def _():
            m2recv[0, :, cols] = jnp.zeros((rows, chunk), jnp.float32)
            m2recv[1, :, cols] = jnp.zeros((rows, chunk), jnp.float32)

        @pl.when(inner)
        def _():
            m2_copy(index).wait_recv()

        def step(place, carry):
            extra, inflow = carry
            layer = layer_at(place)
            above = flux_v[0, pl.ds(layer, 1), :]
            below = flux_v[1, pl.ds(layer, 1), :]
            lateral = jnp.where(row8 == 0, above, jnp.where(row8 == rows - 1, below, 0.0))
            face = face_v[place, :, cols]
            scale = recip(sum_v[place, :, cols] + extra)
            ratio = face * scale
            value = (inflow + (rhs_v[place, :, cols] + lateral)) * scale
            y_v[place, :, cols] = value
            r_v[place, :, cols] = ratio
            return (-(face * ratio), face * value)

        extra, inflow = lax.fori_loop(
            0, layers, step, (m2recv[0, :, cols], m2recv[1, :, cols]), unroll=4
        )
        last = layers - 1
        nsend[0, :, cols] = jnp.where(outer, extra + face_v[last, :, cols], y_v[last, :, cols])
        nsend[1, :, cols] = jnp.where(outer, inflow + last_v[:, cols], r_v[last, :, cols])

        @pl.when(outer)
        def _():
            m2_copy(index).start()

        @pl.when(inner)
        def _():
            m3_copy(index).start()

    def substitute(index, beyond):
        cols = pl.ds(pl.multiple_of(index * chunk, 128), chunk)
        mid = pl.ds(pl.multiple_of(index * chunk + PAD, 128), chunk)

        def step(place, found):
            place = layers - 1 - place
            layer = layer_at(place)
            found = y_v[place, :, cols] + r_v[place, :, cols] * found
            out_v[layer, :, cols] = head_x[layer + 1, :, mid] + found
            return found

        found = lax.fori_loop(0, layers, step, beyond, unroll=4)
        return found

    def finish_inner(index):
        cols = pl.ds(pl.multiple_of(index * chunk, 128), chunk)
        m3_copy(index).wait_recv()
        y_own, r_own = nsend[0, :, cols], nsend[1, :, cols]
        y_far, r_far = m3recv[0, :, cols], m3recv[1, :, cols]
        m4send[:, cols] = substitute(index, (y_far + r_far * y_own) * recip(1.0 - r_own * r_far))
        m4_copy(index).start()

    def finish_outer(index):
        cols = pl.ds(pl.multiple_of(index * chunk, 128), chunk)
        m4_copy(index).wait_recv()
        substitute(index, m4recv[:, cols])

    lag = 5

    def turn(index, carry):
        @pl.when(index < count)
        def _():
            eliminate(index)

        @pl.when(inner & (index >= 2) & (index < count + 2))
        def _():
            finish_inner(index - 2)

        @pl.when(index == jnp.where(outer, count, count + 2))
        def _():
            surface()

        @pl.when(outer & (index >= lag))
        def _():
            finish_outer(index - lag)

        return carry

    lax.fori_loop(0, count + lag, turn, 0)

    def drain(index, carry):
        for side, present in ((0, has_up), (1, has_down)):
            @pl.when(present)
            def _():
                lat_copy(side, index).wait_send()

        @pl.when(outer)
        def _():
            m2_copy(index).wait_send()

        @pl.when(inner)
        def _():
            m3_copy(index).wait_send()
            m4_copy(index).wait_send()
            for copy in m1_sends(index):
                copy.wait_send()

        return carry

    lax.fori_loop(0, count, drain, 0)
    for side, present in ((0, has_up), (1, has_down)):
        @pl.when(present)
        def _():
            surf_copy(side).wait_send()

    @pl.when(is_top)
    def _():
        for target in range(1, 4):
            x_copy(target).wait_send()


def per_device(lat_count, chunk, head, head_old, soil, cond_t, shape_t, pore_t, pond, ground, ponded, river):
    layers, rows, width = head.shape
    chunk = min(chunk, width)
    count = width // chunk
    strip = width // 4
    window = min(strip + 2 * PAD, width)
    f32 = jnp.float32
    padded = (layers + 2, rows, width + 2 * PAD)
    full = (layers, rows, width)
    plane = (rows, width)
    pair = (2, rows, width)
    any_spec = pl.BlockSpec(memory_space=pl.ANY)
    smem = pl.BlockSpec(memory_space=pltpu.SMEM)
    vmem = pl.BlockSpec(memory_space=pltpu.VMEM)
    dma = pltpu.SemaphoreType.DMA
    return pl.pallas_call(
        functools.partial(kernel, (layers, rows, width, lat_count, chunk)),
        out_shape=(pltpu.VMEM(full, f32), pltpu.VMEM((rows, strip), f32)),
        in_specs=[any_spec] * 3 + [smem] * 3 + [vmem] * 4,
        out_specs=(vmem, vmem),
        scratch_shapes=[
            pltpu.VMEM(padded, f32),
            pltpu.VMEM(padded, f32),
            pltpu.VMEM(full, f32),
            pltpu.VMEM(full, jnp.int32),
            pltpu.VMEM(full, f32),
            pltpu.VMEM(full, f32),
            pltpu.VMEM(full, f32),
            pltpu.VMEM(full, f32),
            pltpu.VMEM(full, f32),
            pltpu.VMEM(plane, f32),
            pltpu.VMEM(full, f32),
            pltpu.VMEM(full, f32),
            pltpu.VMEM((2, 2, layers, width), f32),
            pltpu.VMEM((2, 2, layers, width), f32),
            pltpu.VMEM((2, layers, chunk), f32),
            pltpu.VMEM(pair, f32),
            pltpu.VMEM(pair, f32),
            pltpu.VMEM(pair, f32),
            pltpu.VMEM(plane, f32),
            pltpu.VMEM(plane, f32),
            pltpu.VMEM(plane, f32),
            pltpu.VMEM((rows, window), f32),
            pltpu.VMEM((2, 16, window), f32),
            pltpu.VMEM((2, 16, window), f32),
            pltpu.VMEM((4, rows + 8, window), f32),
            pltpu.VMEM((rows, window), f32),
            dma((3, count)),
            dma((2, count)),
            dma((2, count)),
            dma((2, 2, count)),
            dma((2, count)),
            dma((count,)),
            dma((count,)),
            dma((count,)),
            dma((count,)),
            dma((count,)),
            dma((4,)),
            dma(()),
            dma((2,)),
            dma((2,)),
        ],
        compiler_params=pltpu.CompilerParams(
            collective_id=0, has_side_effects=True, vmem_limit_bytes=61 * 1024 * 1024
        ),
    )(head, head_old, soil, cond_t, shape_t, pore_t, pond, ground, ponded, river)


def solution(mesh):
    deep = P("depth", "lat", None)
    flat = P("lat", None)
    return jax.shard_map(
        functools.partial(per_device, mesh.shape["lat"], 512),
        mesh=mesh,
        in_specs=(deep, deep, deep, P(), P(), P(), flat, flat, flat, flat),
        out_specs=(deep, P("lat", "depth")),
        check_vma=False,
    )
```
